32 devices in a mesh: groups: 2 (over x), kv: 16 (over z, y, core).
Axes of the slice: x: 2, y: 2, z: 4, core: 2. Of those that a mesh axis runs over, the one named last changes fastest.
Arguments:
- queries: bfloat16 [64, 8192], P(('groups', 'kv')), parts along dimension 0, may hold values from -48 to 48
- keys: bfloat16 [16384, 1024], P(('groups', 'kv')), parts along dimension 0, may hold values from -6 to 6
- values: bfloat16 [16384, 1024], P(('groups', 'kv')), parts along dimension 0, may hold values from -6 to 6
- block_live: int32 [32, 128], P('groups', 'kv'), parts along dimension 0, may hold values from 0 to 1, as said below
- span_offset: int32 [2], P('groups'), parts along dimension 0, may hold values from 2048 to 7648
Outputs:
- attended: bfloat16 [64, 8192], P(('groups', 'kv')), parts along dimension 0
The draws below stay inside these ranges and needn't reach their ends.
There are 2 independent parts, one for each index of `groups`. The reference program is written for one: setup_inputs(seed, part) draws one part's arguments, and reference() takes and returns one part's arrays. A program takes and returns all parts, laid end to end along the dimension named above; each array names one. Nothing has to cross between parts.
Inputs may be any that keep to these rules, and one draw needn't show every extreme that they name: `block_live`: column 0 is 1 for every query shard.
All inputs are finite; a program needn't handle non-finite values.
Results may differ from the reference program's by a relative error of at most 0.0018.
Values may be sent and summed in bfloat16 or wider, within the bound.
No kernel may reach another device: no remote copies, remote signals or barrier semaphores. Data moves between devices by JAX's collectives and lax.ppermute only.
A program may use at most 128 MiB of HBM per device.

```python
import math
import jax
import jax.numpy as jnp
from jax import lax

H = 64
KVH = 8
HD = 128
BLK = 64
KV_DEV = 512
Q_DEV = 2
GROUP = 8
SEG = 256
CACHE = 8192
Q_TOTAL = 32
QSH = 16
NKB = 128


def draw_keys(key, part):
    cells = jnp.clip(jax.random.normal(jax.random.fold_in(key, 11), (CACHE, KVH * HD), jnp.float32), -6.0, 6.0)
    return cells.astype(jnp.bfloat16)


def draw_queries(key, part):
    cells = 3.0 * jnp.clip(jax.random.normal(jax.random.fold_in(key, 12), (Q_TOTAL, H * HD), jnp.float32), -6.0, 6.0)
    cells = jnp.clip(cells, -48.0, 48.0)
    return cells.astype(jnp.bfloat16)


def draw_block_live(key, part):
    picks = jax.random.randint(jax.random.fold_in(key, 13), (QSH, NKB), 0, 4)
    cells = (picks > 0).astype(jnp.int32)
    return cells.at[:, 0].set(1)


def level_of(key, extent, split, low, high):
    gain, own = 1.0, jax.random.fold_in(key, 6)
    for dim, blocks in split:
        steps = jnp.exp(jax.random.uniform(jax.random.fold_in(own, dim), (blocks,), jnp.float32, low / len(split), high / len(split)))
        gain = gain * jnp.repeat(steps, extent[dim] // blocks).reshape([-1 if axis == dim else 1 for axis in range(len(extent))])
    return gain


def scatter_about(key, shape, spread, most, pieces=(), held_as=jnp.bfloat16):
    drawn = spread * jax.random.normal(key, shape, jnp.float32)
    if pieces:
        drawn = drawn * level_of(key, shape, pieces, -0.22, 0.18)
    return jnp.clip(drawn, -most, most).astype(held_as)


def setup_inputs(seed: int = 0, part: int = 0) -> dict:
    key_list = jax.random.split(jax.random.key(seed), 6)
    own_keys = jax.random.split(jax.random.fold_in(key_list[5], part), 6)
    queries = draw_queries(jax.random.fold_in(jax.random.fold_in(key_list[5], part), 71), part)
    keys = draw_keys(jax.random.fold_in(jax.random.fold_in(key_list[5], part), 71), part)
    values = scatter_about(own_keys[2], (CACHE, KVH * HD), 1.0, 6.0, ((0, 16),))
    block_live = draw_block_live(jax.random.fold_in(jax.random.fold_in(key_list[5], part), 71), part)
    span_offset = jax.random.randint(own_keys[4], (1,), CACHE // 4, CACHE - KV_DEV - Q_TOTAL + 1).astype(jnp.int32)
    return dict(queries=queries, keys=keys, values=values, block_live=block_live, span_offset=span_offset)


SCORE_FLOOR = -30.0

def segment_terms(queries, keys, values, block_live, offset, seg_start):
    queries_four = queries.reshape(Q_TOTAL, KVH, GROUP, HD).astype(jnp.float32)
    key_part = lax.dynamic_slice_in_dim(keys, seg_start, SEG, 0).reshape(SEG, KVH, HD).astype(jnp.float32)
    value_part = lax.dynamic_slice_in_dim(values, seg_start, SEG, 0).reshape(SEG, KVH, HD).astype(jnp.float32)
    scores = jnp.einsum('qgeh,kgh->qgek', queries_four, key_part) * (1.0 / math.sqrt(HD))
    positions = seg_start + jnp.arange(SEG, dtype=jnp.int32)
    queries_at = offset + jnp.arange(Q_TOTAL, dtype=jnp.int32)
    live_cols = lax.dynamic_slice_in_dim(block_live, (seg_start // BLK).astype(jnp.int32), SEG // BLK, 1)
    live_cells = jnp.repeat(jnp.repeat(live_cols, Q_DEV, axis=0), BLK, axis=1) > 0
    allowed = (positions[None, :] <= queries_at[:, None]) & ((positions[None, :] >= offset) | live_cells)
    allowed_four = allowed[:, None, None, :]
    peaks = lax.optimization_barrier(jnp.max(jnp.where(allowed_four, scores, SCORE_FLOOR), axis=3))
    weights = jnp.where(allowed_four, jnp.exp(scores - peaks[..., None]), 0.0)
    totals = lax.optimization_barrier(jnp.sum(weights, axis=3))
    rounded = lax.optimization_barrier(weights.astype(jnp.bfloat16)).astype(jnp.float32)
    partial_out = jnp.einsum('qgek,kgh->qgeh', rounded, value_part)
    return (partial_out.reshape(Q_TOTAL, H * HD), peaks.reshape(Q_TOTAL, H), totals.reshape(Q_TOTAL, H))

def reference(queries, keys, values, block_live, span_offset):
    offset = span_offset[0]
    last_pos = offset + Q_TOTAL - 1

    def nothing(unused):
        return (jnp.zeros((Q_TOTAL, H * HD), jnp.float32), jnp.full((Q_TOTAL, H), SCORE_FLOOR, jnp.float32), jnp.zeros((Q_TOTAL, H), jnp.float32))

    def step(state_now, seg_index):
        weighted, peak_all, total_all = state_now
        seg_start = (seg_index * SEG).astype(jnp.int32)

        def compute(unused):
            return segment_terms(queries, keys, values, block_live, offset, seg_start)
        part_out, part_peak, part_total = lax.cond(seg_start <= last_pos, compute, nothing, 0)
        new_peak = jnp.maximum(peak_all, part_peak)
        old_scale = jnp.exp(peak_all - new_peak)
        new_scale = jnp.exp(part_peak - new_peak)
        weighted = weighted * jnp.repeat(old_scale, HD, axis=1) + part_out * jnp.repeat(new_scale, HD, axis=1)
        total_all = total_all * old_scale + part_total * new_scale
        return ((weighted, new_peak, total_all), 0)
    final_state, unused = lax.scan(step, nothing(0), jnp.arange(CACHE // SEG, dtype=jnp.int32))
    weighted, peak_all, total_all = final_state
    return (weighted / jnp.repeat(total_all, HD, axis=1)).astype(jnp.bfloat16)
```

```python
import functools
import math

import jax
import jax.numpy as jnp
from jax import lax
from jax.experimental import pallas as pl
from jax.experimental.pallas import tpu as pltpu
from jax.sharding import PartitionSpec as P

H = 64
KVH = 8
HD = 128
BLK = 64
GROUP = H // KVH
SCORE_FLOOR = -30.0
ROOT = math.sqrt(HD)
TO_BITS = math.log2(math.e) / ROOT
FIX = 2.0**17
STEPS = 32766.0
NO_WEIGHT = -8191.0
MASKED = -1e30
KINDS = 3
VMEM = pl.BlockSpec(memory_space=pltpu.VMEM)
PARAMS = pltpu.CompilerParams(vmem_limit_bytes=48 * 2**20)


def swap(array, delta):
    count = lax.axis_size("kv")
    return lax.ppermute(array, "kv", [(i, i ^ delta) for i in range(count)])


def exchange_steps(count):
    bits = count.bit_length() - 2
    steps = [[0, 2]]
    bit = 1
    while bit < bits:
        width = min(2, bits - bit)
        steps.append([d << (bit + 1) for d in range(1 << width)])
        bit += width
    return steps[::-1]


def attend_kernel(q_ref, k_ref, vt_ref, bias_ref, *out_refs, segment):
    rows = q_ref.shape[0]
    kv_heads = q_ref.shape[1] // (GROUP * HD)
    segments = k_ref.shape[0] // segment
    chunk = rows // len(out_refs)
    lanes = GROUP * rows
    target = lax.broadcasted_iota(jnp.int32, (HD, lanes), 0)
    head_of = lax.broadcasted_iota(jnp.int32, (HD, lanes), 1) // rows
    stats = jnp.zeros((HD, lanes), jnp.float32)
    for g in range(kv_heads):
        queries = jnp.concatenate(
            [q_ref[:, (g * GROUP + h) * HD : (g * GROUP + h + 1) * HD] for h in range(GROUP)], 0
        )
        peaks, totals, outs = [], [], []
        for s in range(segments):
            at = slice(s * segment, (s + 1) * segment)
            scores = lax.dot_general(
                k_ref[at, g * HD : (g + 1) * HD],
                queries,
                (((1,), (1,)), ((), ())),
                preferred_element_type=jnp.float32,
            )
            scores = scores + bias_ref[at, :]
            peak = jnp.maximum(jnp.max(scores, 0, keepdims=True), SCORE_FLOOR * ROOT)
            weights = jnp.exp2((scores - peak) * TO_BITS)
            peaks.append(peak)
            totals.append(jnp.sum(weights, 0, keepdims=True))
            outs.append(
                jnp.dot(
                    vt_ref[g * HD : (g + 1) * HD, at],
                    weights.astype(jnp.bfloat16),
                    preferred_element_type=jnp.float32,
                )
            )
        top = functools.reduce(jnp.maximum, peaks)
        scales = [jnp.exp2((peak - top) * TO_BITS) for peak in peaks]
        total = sum(e * t for e, t in zip(scales, totals))
        out = sum(e * o for e, o in zip(scales, outs))
        live = total > 0
        safe = jnp.where(live, total, 1.0)
        level = jnp.where(live, top * TO_BITS + jnp.log2(safe), NO_WEIGHT)
        out = out * jnp.where(live, 1.0 / safe, 0.0)
        largest = jnp.max(jnp.abs(out), 0, keepdims=True)
        power = jnp.clip(jnp.ceil(jnp.log2(jnp.maximum(largest, 1e-37))), -100.0, 8.0)
        out = jnp.round((out * (jnp.exp2(-power) * STEPS)).T).astype(jnp.int32).astype(jnp.int16)
        fixed = jnp.round(level * FIX).astype(jnp.int32)
        values = [fixed >> 16, (fixed & 0xFFFF) - 32768, power]
        for kind in range(KINDS):
            stats = jnp.where(
                target == kind * kv_heads * GROUP + g * GROUP + head_of,
                values[kind].astype(jnp.float32),
                stats,
            )
        for h in range(GROUP):
            for c, out_ref in enumerate(out_refs):
                out_ref[:, (g * GROUP + h) * HD : (g * GROUP + h + 1) * HD] = out[
                    h * rows + c * chunk : h * rows + (c + 1) * chunk
                ]
    stats = stats.T
    packed = sum(stats[h * rows : (h + 1) * rows] for h in range(GROUP))
    packed = packed.astype(jnp.int32).astype(jnp.int16)
    for c, out_ref in enumerate(out_refs):
        out_ref[:, kv_heads * GROUP * HD :] = packed[c * chunk : (c + 1) * chunk]


def combine_kernel(*refs, parts, heads, final):
    in_refs, out_refs = refs[:parts], refs[parts:]
    wide = heads * HD
    rows = in_refs[0].shape[0]
    chunk = rows // len(out_refs)
    fixed, powers = [], []
    for ref in in_refs:
        stats = ref[:, wide:].astype(jnp.int32)
        low = pltpu.roll(stats, HD - heads, 1)
        fixed.append((stats << 16) + low + 32768)
        powers.append(pltpu.roll(stats, HD - 2 * heads, 1).astype(jnp.float32))
    top = functools.reduce(jnp.maximum, fixed)
    weights = [jnp.exp2((f - top).astype(jnp.float32) * (1.0 / FIX)) for f in fixed]
    total = sum(weights)
    shares = [w / total for w in weights]
    amounts = [s * jnp.exp2(p) for s, p in zip(shares, powers)]
    if final:
        factors = [a * (1.0 / STEPS) for a in amounts]
    else:
        power = jnp.clip(jnp.ceil(jnp.log2(jnp.maximum(sum(amounts), 1e-37))), -100.0, 8.0)
        back = jnp.exp2(-power)
        factors = [a * back for a in amounts]
    for h in range(heads):
        at = slice(h * HD, (h + 1) * HD)
        out = sum(
            f[:, h : h + 1] * ref[:, at].astype(jnp.int32).astype(jnp.float32)
            for f, ref in zip(factors, in_refs)
        )
        if final:
            out = out.astype(jnp.bfloat16)
        else:
            out = jnp.round(out).astype(jnp.int32).astype(jnp.int16)
        for c, out_ref in enumerate(out_refs):
            out_ref[:, at] = out[c * chunk : (c + 1) * chunk]
    if not final:
        level = top + jnp.round(jnp.log2(total) * FIX).astype(jnp.int32)
        lane = lax.broadcasted_iota(jnp.int32, level.shape, 1)
        high = level >> 16
        low = pltpu.roll((level & 0xFFFF) - 32768, heads, 1)
        power = pltpu.roll(power.astype(jnp.int32), 2 * heads, 1)
        packed = jnp.where(lane < heads, high, jnp.where(lane < 2 * heads, low, power))
        packed = packed.astype(jnp.int16)
        for c, out_ref in enumerate(out_refs):
            out_ref[:, wide:] = packed[c * chunk : (c + 1) * chunk]


def combine(arrays, pieces, heads, final):
    rows = arrays[0].shape[0]
    width = heads * HD if final else arrays[0].shape[1]
    dtype = jnp.bfloat16 if final else jnp.int16
    return pl.pallas_call(
        functools.partial(combine_kernel, parts=len(arrays), heads=heads, final=final),
        out_shape=[jax.ShapeDtypeStruct((rows // pieces, width), dtype)] * pieces,
        in_specs=[VMEM] * len(arrays),
        out_specs=[VMEM] * pieces,
        compiler_params=PARAMS,
    )(*arrays)


def on_device(queries, keys, values, block_live, span_offset):
    count = lax.axis_size("kv")
    me = lax.axis_index("kv")
    core = me % 2
    q_dev, q_width = queries.shape
    kv_dev, kv_width = keys.shape
    segment = kv_dev // 2
    half_q, half_kv = q_width // 2, kv_width // 2
    heads = half_q // HD
    offset = span_offset[0]
    steps = exchange_steps(count)

    def halves(array, half):
        keep = lax.dynamic_slice_in_dim(array, core * half, half, 1)
        send = lax.dynamic_slice_in_dim(array, (1 - core) * half, half, 1)
        return keep, send

    q_keep, q_send = halves(queries, half_q)
    block = jnp.stack([q_keep, swap(q_send, 1)], 0)
    order = [0, 1]
    for deltas in steps:
        block = jnp.concatenate([block] + [swap(block, d) for d in deltas[1:]], 0)
        order = [r ^ d for d in deltas for r in order]
    row_count = count * q_dev
    all_queries = block.reshape(row_count, half_q)

    k_keep, k_send = halves(keys, half_kv)
    v_keep, v_send = halves(values, half_kv)
    k_all = jnp.concatenate([k_keep, swap(k_send, 1)], 0)
    v_all = jnp.concatenate([v_keep, swap(v_send, 1)], 0).T
    live = jnp.concatenate([block_live, swap(block_live, 1)], 1)
    owners = me ^ jnp.array(order, jnp.int32)
    chosen = owners[:, None] == jnp.arange(count, dtype=jnp.int32)[None, :]
    live = jnp.max(jnp.where(chosen[:, :, None], live[None], 0), axis=1)
    live = jnp.repeat(live.T, BLK, axis=0)
    inside = jnp.arange(kv_dev, dtype=jnp.int32)
    positions = jnp.concatenate([me * kv_dev + inside, (me ^ 1) * kv_dev + inside])
    tokens = (owners[:, None] * q_dev + jnp.arange(q_dev, dtype=jnp.int32)[None, :]).reshape(-1)
    allowed = (positions[:, None] <= offset + tokens[None, :]) & (
        (positions[:, None] >= offset) | (jnp.repeat(live, q_dev, axis=1) > 0)
    )
    bias = jnp.tile(jnp.where(allowed, 0.0, MASKED).astype(jnp.float32), (1, GROUP))

    pieces = [len(deltas) for deltas in steps[::-1]] + [2]
    width = half_q + HD
    parts = pl.pallas_call(
        functools.partial(attend_kernel, segment=segment),
        out_shape=[jax.ShapeDtypeStruct((row_count // pieces[0], width), jnp.int16)] * pieces[0],
        in_specs=[VMEM] * 4,
        out_specs=[VMEM] * pieces[0],
        compiler_params=PARAMS,
    )(all_queries, k_all, v_all, bias)
    for stage, deltas in enumerate(steps[::-1]):
        arrays = [parts[0]] + [swap(p, d) for p, d in zip(parts[1:], deltas[1:])]
        last = stage == len(steps) - 1
        parts = combine(arrays, pieces[stage + 1], heads, last)
    keep, send = parts
    other = swap(send, 1)
    return jnp.where(
        core == 0, jnp.concatenate([keep, other], 1), jnp.concatenate([other, keep], 1)
    )


def solution(mesh):
    placed = (
        P(("groups", "kv"), None),
        P(("groups", "kv"), None),
        P(("groups", "kv"), None),
        P("groups", "kv"),
        P("groups"),
    )
    return jax.shard_map(
        on_device, mesh=mesh, in_specs=placed, out_specs=P(("groups", "kv"), None), check_vma=False
    )
```

```python
import functools
import math

import jax
import jax.numpy as jnp
from jax import lax
from jax.experimental import pallas as pl
from jax.experimental.pallas import tpu as pltpu
from jax.sharding import PartitionSpec as P

H = 64
KVH = 8
HD = 128
BLK = 64
GROUP = H // KVH
SCORE_FLOOR = -30.0
ROOT = math.sqrt(HD)
TO_BITS = math.log2(math.e) / ROOT
FIX = 2.0**17
STEPS = 32766.0
NO_WEIGHT = -8191.0
MASKED = -1e30
KINDS = 3
VMEM = pl.BlockSpec(memory_space=pltpu.VMEM)
PARAMS = pltpu.CompilerParams(vmem_limit_bytes=48 * 2**20)


def swap(array, delta):
    count = lax.axis_size("kv")
    return lax.ppermute(array, "kv", [(i, i ^ delta) for i in range(count)])


def exchange_steps(count):
    bits = count.bit_length() - 2
    steps = [[0, 2]]
    bit = 1
    while bit < bits:
        width = min(2, bits - bit)
        steps.append([d << (bit + 1) for d in range(1 << width)])
        bit += width
    return steps[::-1]


def prep_kernel(
    k_own, k_other, v_own, v_other, live_own, live_other, offset_ref, k_all, v_turned, *bias_refs, places
):
    me = lax.axis_index("kv")
    core = me % 2
    kv_dev = k_own.shape[0]
    half = k_all.shape[1]
    count = 2 ** len(places)
    lanes = bias_refs[0].shape[1]
    rows = lanes // GROUP
    q_dev = rows * len(bias_refs) // count
    columns = pl.ds(pl.multiple_of(core * half, half), half)
    offset = offset_ref[0]
    row = lax.broadcasted_iota(jnp.int32, (1, lanes), 1) % rows
    position = lax.broadcasted_iota(jnp.int32, (kv_dev, lanes), 0)
    for side, (k_ref, v_ref, live_ref) in enumerate(
        ((k_own, v_own, live_own), (k_other, v_other, live_other))
    ):
        at = slice(side * kv_dev, (side + 1) * kv_dev)
        k_all[at, :] = k_ref[:, columns]
        v_turned[:, at] = v_ref[:, columns].T
        start = (me ^ side) * kv_dev
        live = live_ref[...].astype(jnp.float32)
        for c, bias_ref in enumerate(bias_refs):
            index = c * (count // len(bias_refs)) + row // q_dev
            owner = me
            for bit, place in enumerate(places):
                owner = owner ^ (((index >> bit) & 1) << place)
            token = owner * q_dev + row % q_dev
            chosen = lax.broadcasted_iota(jnp.int32, (count, lanes), 0) == owner
            seen = jnp.dot(live, chosen.astype(jnp.float32), preferred_element_type=jnp.float32)
            seen = jnp.concatenate(
                [jnp.broadcast_to(seen[b : b + 1], (BLK, lanes)) for b in range(kv_dev // BLK)], 0
            )
            at_key = start + position
            allowed = (at_key <= offset + token) & ((at_key >= offset) | (seen > 0.5))
            bias_ref[at, :] = jnp.where(allowed, 0.0, MASKED)


def attend_kernel(*refs, segment):
    q_refs, (k_ref, vt_ref, bias_ref, out_ref) = refs[:-4], refs[-4:]
    queries_all = jnp.concatenate([ref[...].astype(jnp.float32) for ref in q_refs], 0)
    queries_all = queries_all.astype(jnp.bfloat16)
    rows = queries_all.shape[0]
    kv_heads = queries_all.shape[1] // (GROUP * HD)
    segments = k_ref.shape[0] // segment
    lanes = GROUP * rows
    target = lax.broadcasted_iota(jnp.int32, (HD, lanes), 0)
    head_of = lax.broadcasted_iota(jnp.int32, (HD, lanes), 1) // rows
    stats = jnp.zeros((HD, lanes), jnp.float32)
    for g in range(kv_heads):
        queries = jnp.concatenate(
            [queries_all[:, (g * GROUP + h) * HD : (g * GROUP + h + 1) * HD] for h in range(GROUP)],
            0,
        )
        peaks, totals, outs = [], [], []
        for s in range(segments):
            at = slice(s * segment, (s + 1) * segment)
            scores = lax.dot_general(
                k_ref[at, g * HD : (g + 1) * HD],
                queries,
                (((1,), (1,)), ((), ())),
                preferred_element_type=jnp.float32,
            )
            scores = scores + bias_ref[at, :]
            peak = jnp.maximum(jnp.max(scores, 0, keepdims=True), SCORE_FLOOR * ROOT)
            weights = jnp.exp2((scores - peak) * TO_BITS)
            peaks.append(peak)
            totals.append(jnp.sum(weights, 0, keepdims=True))
            outs.append(
                jnp.dot(
                    vt_ref[g * HD : (g + 1) * HD, at],
                    weights.astype(jnp.bfloat16),
                    preferred_element_type=jnp.float32,
                )
            )
        top = functools.reduce(jnp.maximum, peaks)
        scales = [jnp.exp2((peak - top) * TO_BITS) for peak in peaks]
        total = sum(e * t for e, t in zip(scales, totals))
        out = sum(e * o for e, o in zip(scales, outs))
        live = total > 0
        safe = jnp.where(live, total, 1.0)
        level = jnp.where(live, top * TO_BITS + jnp.log2(safe), NO_WEIGHT)
        out = out * jnp.where(live, 1.0 / safe, 0.0)
        largest = jnp.max(jnp.abs(out), 0, keepdims=True)
        power = jnp.clip(jnp.ceil(jnp.log2(jnp.maximum(largest, 1e-37))), -100.0, 8.0)
        out = jnp.round((out * (jnp.exp2(-power) * STEPS)).T).astype(jnp.int32).astype(jnp.int16)
        fixed = jnp.round(level * FIX).astype(jnp.int32)
        values = [fixed >> 16, (fixed & 0xFFFF) - 32768, power]
        for kind in range(KINDS):
            stats = jnp.where(
                target == kind * kv_heads * GROUP + g * GROUP + head_of,
                values[kind].astype(jnp.float32),
                stats,
            )
        for h in range(GROUP):
            out_ref[:, (g * GROUP + h) * HD : (g * GROUP + h + 1) * HD] = out[h * rows : (h + 1) * rows]
    stats = stats.T
    packed = sum(stats[h * rows : (h + 1) * rows] for h in range(GROUP))
    out_ref[:, kv_heads * GROUP * HD :] = packed.astype(jnp.int32).astype(jnp.int16)


def combine_kernel(*refs, parts, heads, final):
    in_refs, out_refs = refs[:parts], refs[parts:]
    wide = heads * HD
    rows = in_refs[0].shape[0]
    chunk = rows // len(out_refs)
    fixed, powers = [], []
    for ref in in_refs:
        stats = ref[:, wide:].astype(jnp.int32)
        low = pltpu.roll(stats, HD - heads, 1)
        fixed.append((stats << 16) + low + 32768)
        powers.append(pltpu.roll(stats, HD - 2 * heads, 1).astype(jnp.float32))
    top = functools.reduce(jnp.maximum, fixed)
    weights = [jnp.exp2((f - top).astype(jnp.float32) * (1.0 / FIX)) for f in fixed]
    total = sum(weights)
    shares = [w / total for w in weights]
    amounts = [s * jnp.exp2(p) for s, p in zip(shares, powers)]
    if final:
        factors = [a * (1.0 / STEPS) for a in amounts]
    else:
        power = jnp.clip(jnp.ceil(jnp.log2(jnp.maximum(sum(amounts), 1e-37))), -100.0, 8.0)
        back = jnp.exp2(-power)
        factors = [a * back for a in amounts]
    for h in range(heads):
        at = slice(h * HD, (h + 1) * HD)
        out = sum(
            f[:, h : h + 1] * ref[:, at].astype(jnp.int32).astype(jnp.float32)
            for f, ref in zip(factors, in_refs)
        )
        if final:
            out = out.astype(jnp.bfloat16)
        else:
            out = jnp.round(out).astype(jnp.int32).astype(jnp.int16)
        for c, out_ref in enumerate(out_refs):
            out_ref[:, at] = out[c * chunk : (c + 1) * chunk]
    if not final:
        level = top + jnp.round(jnp.log2(total) * FIX).astype(jnp.int32)
        lane = lax.broadcasted_iota(jnp.int32, level.shape, 1)
        high = level >> 16
        low = pltpu.roll((level & 0xFFFF) - 32768, heads, 1)
        power = pltpu.roll(power.astype(jnp.int32), 2 * heads, 1)
        packed = jnp.where(lane < heads, high, jnp.where(lane < 2 * heads, low, power))
        packed = packed.astype(jnp.int16)
        for c, out_ref in enumerate(out_refs):
            out_ref[:, wide:] = packed[c * chunk : (c + 1) * chunk]


def combine(arrays, pieces, heads, final):
    rows = arrays[0].shape[0]
    width = heads * HD if final else arrays[0].shape[1]
    dtype = jnp.bfloat16 if final else jnp.int16
    return pl.pallas_call(
        functools.partial(combine_kernel, parts=len(arrays), heads=heads, final=final),
        out_shape=[jax.ShapeDtypeStruct((rows // pieces, width), dtype)] * pieces,
        in_specs=[VMEM] * len(arrays),
        out_specs=[VMEM] * pieces,
        compiler_params=PARAMS,
    )(*arrays)


def on_device(queries, keys, values, block_live, span_offset):
    count = lax.axis_size("kv")
    core = lax.axis_index("kv") % 2
    q_dev, q_width = queries.shape
    kv_dev, kv_width = keys.shape
    half_q, half_kv = q_width // 2, kv_width // 2
    heads = half_q // HD
    steps = exchange_steps(count)

    both = jnp.concatenate([queries, swap(queries, 1)], 0)
    pieces = [lax.dynamic_slice_in_dim(both, core * half_q, half_q, 1)]
    places = [0]
    for deltas in steps:
        moved = [swap(p, d) for d in deltas[1:] for p in pieces]
        pieces = pieces + moved
        places += [(deltas[1] << b).bit_length() - 1 for b in range(len(deltas).bit_length() - 1)]
    parts = len(steps[-1])
    row_count = count * q_dev
    chunk = row_count // parts

    k_all, v_turned, *biases = pl.pallas_call(
        functools.partial(prep_kernel, places=places),
        out_shape=[
            jax.ShapeDtypeStruct((2 * kv_dev, half_kv), keys.dtype),
            jax.ShapeDtypeStruct((half_kv, 2 * kv_dev), keys.dtype),
        ]
        + [jax.ShapeDtypeStruct((2 * kv_dev, chunk * GROUP), jnp.float32)] * parts,
        in_specs=[VMEM] * 6 + [pl.BlockSpec(memory_space=pltpu.SMEM)],
        out_specs=[VMEM] * (2 + parts),
        compiler_params=PARAMS,
        cost_estimate=pl.CostEstimate(flops=0, bytes_accessed=8 * 2**20, transcendentals=0),
    )(
        keys, swap(keys, 1), values, swap(values, 1), block_live.T, swap(block_live, 1).T, span_offset
    )
    outs = []
    for c in range(parts):
        mine = pieces[c * len(pieces) // parts : (c + 1) * len(pieces) // parts]
        outs.append(
            pl.pallas_call(
                functools.partial(attend_kernel, segment=kv_dev // 2),
                out_shape=jax.ShapeDtypeStruct((chunk, half_q + HD), jnp.int16),
                in_specs=[VMEM] * (len(mine) + 3),
                out_specs=VMEM,
                compiler_params=PARAMS,
                cost_estimate=pl.CostEstimate(
                    flops=4 * chunk * half_q * 2 * kv_dev,
                    bytes_accessed=6 * 2**20,
                    transcendentals=chunk * heads * 2 * kv_dev,
                ),
            )(*mine, k_all, v_turned, biases[c])
        )
    splits = [len(deltas) for deltas in steps[::-1]] + [2]
    for stage, deltas in enumerate(steps[::-1]):
        arrays = [outs[0]] + [swap(p, d) for p, d in zip(outs[1:], deltas[1:])]
        outs = combine(arrays, splits[stage + 1], heads, stage == len(steps) - 1)
    keep, send = outs
    other = swap(send, 1)
    return jnp.where(
        core == 0, jnp.concatenate([keep, other], 1), jnp.concatenate([other, keep], 1)
    )


def solution(mesh):
    placed = (
        P(("groups", "kv"), None),
        P(("groups", "kv"), None),
        P(("groups", "kv"), None),
        P("groups", "kv"),
        P("groups"),
    )
    return jax.shard_map(
        on_device, mesh=mesh, in_specs=placed, out_specs=P(("groups", "kv"), None), check_vma=False
    )
```

```python
import functools
import math

import jax
import jax.numpy as jnp
from jax import lax
from jax.experimental import pallas as pl
from jax.experimental.pallas import tpu as pltpu
from jax.sharding import PartitionSpec as P

H = 64
KVH = 8
HD = 128
BLK = 64
GROUP = H // KVH
SCORE_FLOOR = -30.0
ROOT = math.sqrt(HD)
TO_BITS = math.log2(math.e) / ROOT
FIX = 2.0**17
STEPS = 32766.0
NO_WEIGHT = -8191.0
MASKED = -1e30
KINDS = 3
SLOT = HD // 2
STATS = 2 * HD
VMEM = pl.BlockSpec(memory_space=pltpu.VMEM)
PARAMS = pltpu.CompilerParams(vmem_limit_bytes=24 * 2**20)


def swap(array, delta):
    count = lax.axis_size("kv")
    return lax.ppermute(array, "kv", [(i, i ^ delta) for i in range(count)])


def exchange_steps(count):
    bits = count.bit_length() - 1
    steps = [[0, 1], [0, 2]]
    bit = 2
    while bit < bits:
        width = min(2, bits - bit)
        steps.append([d << bit for d in range(1 << width)])
        bit += width
    return steps[::-1]


def prep_kernel(v_ref, live_ref, offset_ref, v_turned, *bias_refs, places):
    me = lax.axis_index("kv")
    kv_dev = v_ref.shape[0]
    count = 2 ** len(places)
    lanes = bias_refs[0].shape[1]
    rows = lanes // GROUP
    q_dev = rows * len(bias_refs) // count
    offset = offset_ref[0]
    row = lax.broadcasted_iota(jnp.int32, (1, lanes), 1) % rows
    at_key = me * kv_dev + lax.broadcasted_iota(jnp.int32, (kv_dev, lanes), 0)
    live = live_ref[...].astype(jnp.float32)
    for c, bias_ref in enumerate(bias_refs):
        index = c * (count // len(bias_refs)) + row // q_dev
        owner = me
        for bit, place in enumerate(places):
            owner = owner ^ (((index >> bit) & 1) << place)
        token = owner * q_dev + row % q_dev
        chosen = lax.broadcasted_iota(jnp.int32, (count, lanes), 0) == owner
        seen = jnp.dot(live, chosen.astype(jnp.float32), preferred_element_type=jnp.float32)
        seen = jnp.concatenate(
            [jnp.broadcast_to(seen[b : b + 1], (BLK, lanes)) for b in range(kv_dev // BLK)], 0
        )
        allowed = (at_key <= offset + token) & ((at_key >= offset) | (seen > 0.5))
        bias_ref[...] = jnp.where(allowed, 0.0, MASKED)
    v_turned[...] = v_ref[...].T


def join_kernel(*refs):
    *in_refs, out_ref = refs
    joined = jnp.concatenate([ref[...].astype(jnp.float32) for ref in in_refs], 0)
    out_ref[...] = joined.astype(out_ref.dtype)


def join(pieces):
    rows, width = pieces[0].shape
    return pl.pallas_call(
        join_kernel,
        out_shape=jax.ShapeDtypeStruct((len(pieces) * rows, width), pieces[0].dtype),
        in_specs=[VMEM] * len(pieces),
        out_specs=VMEM,
        compiler_params=PARAMS,
    )(*pieces)


def attend_kernel(*refs, segment):
    *q_refs, k_ref, vt_ref, bias_ref, out_ref = refs
    queries_all = jnp.concatenate([ref[...] for ref in q_refs], 0)
    rows, width = queries_all.shape
    kv_heads = width // (GROUP * HD)
    segments = k_ref.shape[0] // segment
    lanes = GROUP * rows
    target = lax.broadcasted_iota(jnp.int32, (STATS, lanes), 0)
    head_of = lax.broadcasted_iota(jnp.int32, (STATS, lanes), 1) // rows
    stats = jnp.zeros((STATS, lanes), jnp.float32)
    for g in range(kv_heads):
        queries = jnp.concatenate(
            [queries_all[:, (g * GROUP + h) * HD : (g * GROUP + h + 1) * HD] for h in range(GROUP)],
            0,
        )
        peaks, totals, outs = [], [], []
        for s in range(segments):
            at = slice(s * segment, (s + 1) * segment)
            scores = lax.dot_general(
                k_ref[at, g * HD : (g + 1) * HD],
                queries,
                (((1,), (1,)), ((), ())),
                preferred_element_type=jnp.float32,
            )
            scores = scores + bias_ref[at, :]
            peak = jnp.maximum(jnp.max(scores, 0, keepdims=True), SCORE_FLOOR * ROOT)
            weights = jnp.exp2((scores - peak) * TO_BITS)
            peaks.append(peak)
            totals.append(jnp.sum(weights, 0, keepdims=True))
            outs.append(
                jnp.dot(
                    vt_ref[g * HD : (g + 1) * HD, at],
                    weights.astype(jnp.bfloat16),
                    preferred_element_type=jnp.float32,
                )
            )
        top = functools.reduce(jnp.maximum, peaks)
        scales = [jnp.exp2((peak - top) * TO_BITS) for peak in peaks]
        total = sum(e * t for e, t in zip(scales, totals))
        out = sum(e * o for e, o in zip(scales, outs))
        live = total > 0
        safe = jnp.where(live, total, 1.0)
        level = jnp.where(live, top * TO_BITS + jnp.log2(safe), NO_WEIGHT)
        out = out * jnp.where(live, 1.0 / safe, 0.0)
        largest = jnp.max(jnp.abs(out), 0, keepdims=True)
        power = jnp.clip(jnp.ceil(jnp.log2(jnp.maximum(largest, 1e-37))), -100.0, 8.0)
        out = jnp.round((out * (jnp.exp2(-power) * STEPS)).T).astype(jnp.int32).astype(jnp.int16)
        fixed = jnp.round(level * FIX).astype(jnp.int32)
        values = [fixed >> 16, (fixed & 0xFFFF) - 32768, power]
        for kind in range(KINDS):
            stats = jnp.where(
                target == kind * SLOT + g * GROUP + head_of,
                values[kind].astype(jnp.float32),
                stats,
            )
        for h in range(GROUP):
            out_ref[:, (g * GROUP + h) * HD : (g * GROUP + h + 1) * HD] = out[h * rows : (h + 1) * rows]
    stats = stats.T
    packed = sum(stats[h * rows : (h + 1) * rows] for h in range(GROUP))
    out_ref[:, kv_heads * GROUP * HD :] = packed.astype(jnp.int32).astype(jnp.int16)


def combine_kernel(*refs, parts, heads, final):
    in_refs, out_refs = refs[:parts], refs[parts:]
    wide = heads * HD
    rows = in_refs[0].shape[0]
    chunk = rows // len(out_refs)
    fixed, powers = [], []
    for ref in in_refs:
        stats = ref[:, wide : wide + HD].astype(jnp.int32)
        fixed.append((stats << 16) + pltpu.roll(stats, SLOT, 1) + 32768)
        powers.append(ref[:, wide + HD :].astype(jnp.int32).astype(jnp.float32))
    top = functools.reduce(jnp.maximum, fixed)
    weights = [jnp.exp2((f - top).astype(jnp.float32) * (1.0 / FIX)) for f in fixed]
    total = sum(weights)
    shares = [w / total for w in weights]
    amounts = [s * jnp.exp2(p) for s, p in zip(shares, powers)]
    if final:
        factors = [a * (1.0 / STEPS) for a in amounts]
    else:
        power = jnp.clip(jnp.ceil(jnp.log2(jnp.maximum(sum(amounts), 1e-37))), -100.0, 8.0)
        back = jnp.exp2(-power)
        factors = [a * back for a in amounts]
    for h in range(heads):
        at = slice(h * HD, (h + 1) * HD)
        out = sum(
            f[:, h : h + 1] * ref[:, at].astype(jnp.int32).astype(jnp.float32)
            for f, ref in zip(factors, in_refs)
        )
        if final:
            out = out.astype(jnp.bfloat16)
        else:
            out = jnp.round(out).astype(jnp.int32).astype(jnp.int16)
        for c, out_ref in enumerate(out_refs):
            out_ref[:, at] = out[c * chunk : (c + 1) * chunk]
    if not final:
        level = top + jnp.round(jnp.log2(total) * FIX).astype(jnp.int32)
        lane = lax.broadcasted_iota(jnp.int32, level.shape, 1)
        low = pltpu.roll((level & 0xFFFF) - 32768, SLOT, 1)
        packed = jnp.concatenate(
            [jnp.where(lane < SLOT, level >> 16, low), power.astype(jnp.int32)], 1
        )
        packed = packed.astype(jnp.int16)
        for c, out_ref in enumerate(out_refs):
            out_ref[:, wide:] = packed[c * chunk : (c + 1) * chunk]


def combine(arrays, pieces, heads, final):
    rows = arrays[0].shape[0]
    width = heads * HD if final else arrays[0].shape[1]
    dtype = jnp.bfloat16 if final else jnp.int16
    return pl.pallas_call(
        functools.partial(combine_kernel, parts=len(arrays), heads=heads, final=final),
        out_shape=[jax.ShapeDtypeStruct((rows // pieces, width), dtype)] * pieces,
        in_specs=[VMEM] * len(arrays),
        out_specs=[VMEM] * pieces,
        compiler_params=PARAMS,
    )(*arrays)


def on_device(queries, keys, values, block_live, span_offset):
    count = lax.axis_size("kv")
    q_dev, q_width = queries.shape
    kv_dev, kv_width = keys.shape
    heads = q_width // HD
    steps = exchange_steps(count)
    places = []
    for deltas in steps:
        places += [(deltas[1] << b).bit_length() - 1 for b in range(len(deltas).bit_length() - 1)]
    parts = len(steps[-1])
    chunk = count * q_dev // parts

    prepared = pl.pallas_call(
        functools.partial(prep_kernel, places=places),
        out_shape=[jax.ShapeDtypeStruct((kv_width, kv_dev), values.dtype)]
        + [jax.ShapeDtypeStruct((kv_dev, chunk * GROUP), jnp.float32)] * parts,
        in_specs=[VMEM] * 2 + [pl.BlockSpec(memory_space=pltpu.SMEM)],
        out_specs=[VMEM] * (1 + parts),
        compiler_params=PARAMS,
        cost_estimate=pl.CostEstimate(flops=0, bytes_accessed=4 * 2**20, transcendentals=0),
    )(values, block_live.T, span_offset)

    block = queries
    for stage, deltas in enumerate(steps[:-2]):
        others = [swap(block, d) for d in reversed(deltas[1:])][::-1]
        if stage == 0:
            block, others, prepared = lax.optimization_barrier((block, others, prepared))
        block = join([block] + others)
    v_turned, *biases = prepared
    pieces = [block]
    for deltas in steps[-2:]:
        pieces = pieces + [swap(p, d) for d in deltas[1:] for p in pieces]

    def attend(pieces, bias):
        return pl.pallas_call(
            functools.partial(attend_kernel, segment=kv_dev // 2),
            out_shape=jax.ShapeDtypeStruct((chunk, q_width + STATS), jnp.int16),
            in_specs=[VMEM] * (len(pieces) + 3),
            out_specs=VMEM,
            compiler_params=PARAMS,
            cost_estimate=pl.CostEstimate(
                flops=4 * chunk * q_width * kv_dev,
                bytes_accessed=4 * 2**20,
                transcendentals=chunk * heads * kv_dev,
            ),
        )(*pieces, keys, v_turned, bias)

    share = len(pieces) // parts
    first = attend(pieces[:share], biases[0])
    *others, first = lax.optimization_barrier((*pieces[share:], first))
    outs = [first] + [
        attend(others[c * share : (c + 1) * share], biases[c + 1]) for c in range(parts - 1)
    ]
    splits = [len(deltas) for deltas in steps[::-1]] + [1]
    for stage, deltas in enumerate(steps[::-1]):
        sent = [swap(p, d) for p, d in zip(outs[:0:-1], deltas[:0:-1])]
        arrays = [outs[0]] + sent[::-1]
        outs = combine(arrays, splits[stage + 1], heads, stage == len(steps) - 1)
    return outs[0]


def solution(mesh):
    placed = (
        P(("groups", "kv"), None),
        P(("groups", "kv"), None),
        P(("groups", "kv"), None),
        P("groups", "kv"),
        P("groups"),
    )
    return jax.shard_map(
        on_device, mesh=mesh, in_specs=placed, out_specs=P(("groups", "kv"), None), check_vma=False
    )
```

```python
import functools
import math

import jax
import jax.numpy as jnp
from jax import lax
from jax.experimental import pallas as pl
from jax.experimental.pallas import tpu as pltpu
from jax.sharding import PartitionSpec as P

H = 64
KVH = 8
HD = 128
BLK = 64
GROUP = H // KVH
SCORE_FLOOR = -30.0
ROOT = math.sqrt(HD)
TO_BITS = math.log2(math.e) / ROOT
FIX = 2.0**17
STEPS = 32766.0
NO_WEIGHT = -8191.0
MASKED = -1e30
KINDS = 3
SLOT = HD // 2
STATS = 2 * HD
VMEM = pl.BlockSpec(memory_space=pltpu.VMEM)
PARAMS = pltpu.CompilerParams(vmem_limit_bytes=24 * 2**20)


def swap(array, delta):
    count = lax.axis_size("kv")
    return lax.ppermute(array, "kv", [(i, i ^ delta) for i in range(count)])


def exchange_steps(count):
    bits = count.bit_length() - 1
    steps = [[0, 1], [0, 2]]
    bit = 2
    while bit < bits:
        width = min(2, bits - bit)
        steps.append([d << bit for d in range(1 << width)])
        bit += width
    return steps[::-1]


def prep_kernel(v_ref, live_ref, offset_ref, v_turned, *bias_refs, places):
    me = lax.axis_index("kv")
    kv_dev = v_ref.shape[0]
    count = 2 ** len(places)
    lanes = bias_refs[0].shape[1]
    rows = lanes // GROUP
    q_dev = rows * len(bias_refs) // count
    offset = offset_ref[0]
    row = lax.broadcasted_iota(jnp.int32, (1, lanes), 1) % rows
    at_key = me * kv_dev + lax.broadcasted_iota(jnp.int32, (kv_dev, lanes), 0)
    live = live_ref[...].astype(jnp.float32)
    for c, bias_ref in enumerate(bias_refs):
        index = c * (count // len(bias_refs)) + row // q_dev
        owner = me
        for bit, place in enumerate(places):
            owner = owner ^ (((index >> bit) & 1) << place)
        token = owner * q_dev + row % q_dev
        chosen = lax.broadcasted_iota(jnp.int32, (count, lanes), 0) == owner
        seen = jnp.dot(live, chosen.astype(jnp.float32), preferred_element_type=jnp.float32)
        seen = jnp.concatenate(
            [jnp.broadcast_to(seen[b : b + 1], (BLK, lanes)) for b in range(kv_dev // BLK)], 0
        )
        allowed = (at_key <= offset + token) & ((at_key >= offset) | (seen > 0.5))
        bias_ref[...] = jnp.where(allowed, 0.0, MASKED)
    v_turned[...] = v_ref[...].T


def join_kernel(*refs):
    *in_refs, out_ref = refs
    joined = jnp.concatenate([ref[...].astype(jnp.float32) for ref in in_refs], 0)
    out_ref[...] = joined.astype(out_ref.dtype)


def join(pieces):
    rows, width = pieces[0].shape
    return pl.pallas_call(
        join_kernel,
        out_shape=jax.ShapeDtypeStruct((len(pieces) * rows, width), pieces[0].dtype),
        in_specs=[VMEM] * len(pieces),
        out_specs=VMEM,
        compiler_params=PARAMS,
    )(*pieces)


def attend_kernel(*refs, segment, first):
    *q_refs, k_ref, vt_ref, bias_ref, out_ref = refs
    width = out_ref.shape[1] - STATS
    start = first * GROUP * HD
    queries_all = jnp.concatenate([ref[:, start : start + width] for ref in q_refs], 0)
    rows = queries_all.shape[0]
    kv_heads = width // (GROUP * HD)
    segments = k_ref.shape[0] // segment
    lanes = GROUP * rows
    target = lax.broadcasted_iota(jnp.int32, (STATS, lanes), 0)
    head_of = lax.broadcasted_iota(jnp.int32, (STATS, lanes), 1) // rows
    stats = jnp.zeros((STATS, lanes), jnp.float32)
    for g in range(kv_heads):
        queries = jnp.concatenate(
            [queries_all[:, (g * GROUP + h) * HD : (g * GROUP + h + 1) * HD] for h in range(GROUP)],
            0,
        )
        peaks, totals, outs = [], [], []
        for s in range(segments):
            at = slice(s * segment, (s + 1) * segment)
            scores = lax.dot_general(
                k_ref[at, (first + g) * HD : (first + g + 1) * HD],
                queries,
                (((1,), (1,)), ((), ())),
                preferred_element_type=jnp.float32,
            )
            scores = scores + bias_ref[at, :]
            peak = jnp.maximum(jnp.max(scores, 0, keepdims=True), SCORE_FLOOR * ROOT)
            weights = jnp.exp2((scores - peak) * TO_BITS)
            peaks.append(peak)
            totals.append(jnp.sum(weights, 0, keepdims=True))
            outs.append(
                jnp.dot(
                    vt_ref[(first + g) * HD : (first + g + 1) * HD, at],
                    weights.astype(jnp.bfloat16),
                    preferred_element_type=jnp.float32,
                )
            )
        top = functools.reduce(jnp.maximum, peaks)
        scales = [jnp.exp2((peak - top) * TO_BITS) for peak in peaks]
        total = sum(e * t for e, t in zip(scales, totals))
        out = sum(e * o for e, o in zip(scales, outs))
        live = total > 0
        safe = jnp.where(live, total, 1.0)
        level = jnp.where(live, top * TO_BITS + jnp.log2(safe), NO_WEIGHT)
        out = out * jnp.where(live, 1.0 / safe, 0.0)
        largest = jnp.max(jnp.abs(out), 0, keepdims=True)
        power = jnp.clip(jnp.ceil(jnp.log2(jnp.maximum(largest, 1e-37))), -100.0, 8.0)
        out = jnp.round((out * (jnp.exp2(-power) * STEPS)).T).astype(jnp.int32).astype(jnp.int16)
        fixed = jnp.round(level * FIX).astype(jnp.int32)
        values = [fixed >> 16, (fixed & 0xFFFF) - 32768, power]
        for kind in range(KINDS):
            stats = jnp.where(
                target == kind * SLOT + (first + g) * GROUP + head_of,
                values[kind].astype(jnp.float32),
                stats,
            )
        for h in range(GROUP):
            out_ref[:, (g * GROUP + h) * HD : (g * GROUP + h + 1) * HD] = out[h * rows : (h + 1) * rows]
    stats = stats.T
    packed = sum(stats[h * rows : (h + 1) * rows] for h in range(GROUP))
    out_ref[:, kv_heads * GROUP * HD :] = packed.astype(jnp.int32).astype(jnp.int16)


def combine_kernel(*refs, layout, heads, final):
    wide = heads * HD
    sources = []
    for number in layout:
        sources.append(refs[:number])
        refs = refs[number:]
    out_refs = refs
    rows = sources[0][0].shape[0]
    chunk = rows // len(out_refs)
    fixed, powers = [], []
    for source in sources:
        stats = sum(ref[:, wide // len(source) :].astype(jnp.int32) for ref in source)
        level = stats[:, :HD]
        fixed.append((level << 16) + pltpu.roll(level, SLOT, 1) + 32768)
        powers.append(stats[:, HD:].astype(jnp.float32))
    top = functools.reduce(jnp.maximum, fixed)
    weights = [jnp.exp2((f - top).astype(jnp.float32) * (1.0 / FIX)) for f in fixed]
    total = sum(weights)
    shares = [w / total for w in weights]
    amounts = [s * jnp.exp2(p) for s, p in zip(shares, powers)]
    if final:
        factors = [a * (1.0 / STEPS) for a in amounts]
    else:
        power = jnp.clip(jnp.ceil(jnp.log2(jnp.maximum(sum(amounts), 1e-37))), -100.0, 8.0)
        back = jnp.exp2(-power)
        factors = [a * back for a in amounts]
    for h in range(heads):
        at = slice(h * HD, (h + 1) * HD)
        values = []
        for source in sources:
            share = heads // len(source)
            ref, local = source[h // share], h % share
            values.append(ref[:, local * HD : (local + 1) * HD].astype(jnp.int32))
        out = sum(f[:, h : h + 1] * v.astype(jnp.float32) for f, v in zip(factors, values))
        if final:
            out = out.astype(jnp.bfloat16)
        else:
            out = jnp.round(out).astype(jnp.int32).astype(jnp.int16)
        for c, out_ref in enumerate(out_refs):
            out_ref[:, at] = out[c * chunk : (c + 1) * chunk]
    if not final:
        level = top + jnp.round(jnp.log2(total) * FIX).astype(jnp.int32)
        lane = lax.broadcasted_iota(jnp.int32, level.shape, 1)
        low = pltpu.roll((level & 0xFFFF) - 32768, SLOT, 1)
        packed = jnp.concatenate(
            [jnp.where(lane < SLOT, level >> 16, low), power.astype(jnp.int32)], 1
        )
        packed = packed.astype(jnp.int16)
        for c, out_ref in enumerate(out_refs):
            out_ref[:, wide:] = packed[c * chunk : (c + 1) * chunk]


def combine(sources, pieces, heads, final):
    rows = sources[0][0].shape[0]
    width = heads * HD + (0 if final else STATS)
    dtype = jnp.bfloat16 if final else jnp.int16
    arrays = [array for source in sources for array in source]
    return pl.pallas_call(
        functools.partial(
            combine_kernel, layout=[len(source) for source in sources], heads=heads, final=final
        ),
        out_shape=[jax.ShapeDtypeStruct((rows // pieces, width), dtype)] * pieces,
        in_specs=[VMEM] * len(arrays),
        out_specs=[VMEM] * pieces,
        compiler_params=PARAMS,
    )(*arrays)


def fetch_kernel(in_ref, out_ref, sem):
    copy = pltpu.make_async_copy(in_ref, out_ref, sem)
    copy.start()
    copy.wait()


def fetch(array):
    return pl.pallas_call(
        fetch_kernel,
        out_shape=jax.ShapeDtypeStruct(array.shape, array.dtype),
        in_specs=[pl.BlockSpec(memory_space=pl.ANY)],
        out_specs=VMEM,
        scratch_shapes=[pltpu.SemaphoreType.DMA],
        compiler_params=PARAMS,
    )(array)


def on_device(queries, keys, values, block_live, span_offset):
    count = lax.axis_size("kv")
    q_dev, q_width = queries.shape
    kv_dev, kv_width = keys.shape
    heads = q_width // HD
    steps = exchange_steps(count)
    places = []
    for deltas in steps:
        places += [(deltas[1] << b).bit_length() - 1 for b in range(len(deltas).bit_length() - 1)]
    parts = len(steps[-1])
    chunk = count * q_dev // parts

    prepared = pl.pallas_call(
        functools.partial(prep_kernel, places=places),
        out_shape=[jax.ShapeDtypeStruct((kv_width, kv_dev), values.dtype)]
        + [jax.ShapeDtypeStruct((kv_dev, chunk * GROUP), jnp.float32)] * parts,
        in_specs=[VMEM] * 2 + [pl.BlockSpec(memory_space=pltpu.SMEM)],
        out_specs=[VMEM] * (1 + parts),
        compiler_params=PARAMS,
        cost_estimate=pl.CostEstimate(flops=0, bytes_accessed=4 * 2**20, transcendentals=0),
    )(values, block_live.T, span_offset)

    block = queries
    for stage, deltas in enumerate(steps[:-2]):
        others = [swap(block, d) for d in deltas[2:] + deltas[1:2]]
        if stage == 0:
            others, block = lax.optimization_barrier((others, fetch(block)))
        block = join([block] + others[-1:] + others[:-1])
    pieces = [block]
    for deltas in steps[-2:]:
        moved = [swap(p, d) for d in deltas[1:] for p in pieces]
        if deltas is steps[-2]:
            moved, prepared = lax.optimization_barrier((moved, prepared))
        pieces = pieces + moved
    v_turned, *biases = prepared

    def attend(pieces, bias, part, cuts):
        width = q_width // cuts
        return pl.pallas_call(
            functools.partial(
                attend_kernel, segment=kv_dev // 2, first=part * (heads // GROUP // cuts)
            ),
            out_shape=jax.ShapeDtypeStruct((chunk, width + STATS), jnp.int16),
            in_specs=[VMEM] * (len(pieces) + 3),
            out_specs=VMEM,
            compiler_params=PARAMS,
            cost_estimate=pl.CostEstimate(
                flops=4 * chunk * width * kv_dev,
                bytes_accessed=4 * 2**20 // cuts,
                transcendentals=chunk * width // HD * kv_dev,
            ),
        )(*pieces, keys, v_turned, bias)

    share = len(pieces) // parts
    early = attend(pieces[:share], biases[0], 0, 2)
    *others, early = lax.optimization_barrier((*pieces[share:], early))
    late = [
        attend(others[c * share : (c + 1) * share], biases[c + 1], 0, 1) for c in range(parts - 1)
    ]
    outs = [early] + late
    splits = [len(deltas) for deltas in steps[::-1]] + [1]
    for stage, deltas in enumerate(steps[::-1]):
        sources = [[swap(p, d)] for p, d in zip(outs[:0:-1], deltas[:0:-1])]
        own = [outs[0]]
        if stage == 0:
            own.append(attend(pieces[:share], biases[0], 1, 2))
            own[1], sources = lax.optimization_barrier((own[1], sources))
        outs = combine([own] + sources, splits[stage + 1], heads, stage == len(steps) - 1)
    return outs[0]


def solution(mesh):
    placed = (
        P(("groups", "kv"), None),
        P(("groups", "kv"), None),
        P(("groups", "kv"), None),
        P("groups", "kv"),
        P("groups"),
    )
    return jax.shard_map(
        on_device, mesh=mesh, in_specs=placed, out_specs=P(("groups", "kv"), None), check_vma=False
    )
```

```python
import functools
import math

import jax
import jax.numpy as jnp
from jax import lax
from jax.experimental import pallas as pl
from jax.experimental.pallas import tpu as pltpu
from jax.sharding import PartitionSpec as P

H = 64
KVH = 8
HD = 128
BLK = 64
GROUP = H // KVH
SCORE_FLOOR = -30.0
ROOT = math.sqrt(HD)
TO_BITS = math.log2(math.e) / ROOT
FIX = 2.0**17
STEPS = 32766.0
NO_WEIGHT = -8191.0
MASKED = -1e30
AHEAD = 1
KINDS = 3
SLOT = HD // 2
STATS = 2 * HD
KV_SLOT = SLOT // GROUP
VMEM = pl.BlockSpec(memory_space=pltpu.VMEM)
PARAMS = pltpu.CompilerParams(vmem_limit_bytes=24 * 2**20)


def swap(array, delta):
    count = lax.axis_size("kv")
    return lax.ppermute(array, "kv", [(i, i ^ delta) for i in range(count)])


def exchange_steps(count):
    bits = count.bit_length() - 1
    steps = [[0, 1], [0, 2]]
    bit = 2
    while bit < bits:
        width = min(2, bits - bit)
        steps.append([d << bit for d in range(1 << width)])
        bit += width
    return steps[::-1]


def prep_kernel(v_ref, live_ref, offset_ref, v_turned, *bias_refs, places):
    me = lax.axis_index("kv")
    kv_dev = v_ref.shape[0]
    count = 2 ** len(places)
    lanes = bias_refs[0].shape[1]
    rows = lanes // GROUP
    q_dev = rows * len(bias_refs) // count
    offset = offset_ref[0]
    row = lax.broadcasted_iota(jnp.int32, (1, lanes), 1) % rows
    at_key = me * kv_dev + lax.broadcasted_iota(jnp.int32, (kv_dev, lanes), 0)
    live = live_ref[...].astype(jnp.float32)
    for c, bias_ref in enumerate(bias_refs):
        index = c * (count // len(bias_refs)) + row // q_dev
        owner = me
        for bit, place in enumerate(places):
            owner = owner ^ (((index >> bit) & 1) << place)
        token = owner * q_dev + row % q_dev
        chosen = lax.broadcasted_iota(jnp.int32, (count, lanes), 0) == owner
        seen = jnp.dot(live, chosen.astype(jnp.float32), preferred_element_type=jnp.float32)
        seen = jnp.concatenate(
            [jnp.broadcast_to(seen[b : b + 1], (BLK, lanes)) for b in range(kv_dev // BLK)], 0
        )
        allowed = (at_key <= offset + token) & ((at_key >= offset) | (seen > 0.5))
        bias_ref[...] = jnp.where(allowed, 0.0, MASKED)
    v_turned[...] = v_ref[...].T


def join_kernel(*refs):
    *in_refs, out_ref = refs
    joined = jnp.concatenate([ref[...].astype(jnp.float32) for ref in in_refs], 0)
    out_ref[...] = joined.astype(out_ref.dtype)


def join(pieces):
    rows, width = pieces[0].shape
    return pl.pallas_call(
        join_kernel,
        out_shape=jax.ShapeDtypeStruct((len(pieces) * rows, width), pieces[0].dtype),
        in_specs=[VMEM] * len(pieces),
        out_specs=VMEM,
        compiler_params=PARAMS,
    )(*pieces)


def attend_kernel(*refs, segment, first):
    *q_refs, k_ref, vt_ref, bias_ref, out_ref = refs
    width = out_ref.shape[1] - STATS
    start = first * GROUP * HD
    queries_all = jnp.concatenate([ref[:, start : start + width] for ref in q_refs], 0)
    rows = queries_all.shape[0]
    kv_heads = width // (GROUP * HD)
    segments = k_ref.shape[0] // segment
    lanes = GROUP * rows
    stats = [[jnp.zeros((1, lanes), jnp.float32)] * KV_SLOT for _ in range(KINDS)]
    tiles = [(g, s) for g in range(kv_heads) for s in range(segments)]
    queries = {}

    def score(g, s):
        if g not in queries:
            queries[g] = jnp.concatenate(
                [
                    queries_all[:, (g * GROUP + h) * HD : (g * GROUP + h + 1) * HD]
                    for h in range(GROUP)
                ],
                0,
            )
        at = slice(s * segment, (s + 1) * segment)
        scores = lax.dot_general(
            k_ref[at, (first + g) * HD : (first + g + 1) * HD],
            queries[g],
            (((1,), (1,)), ((), ())),
            preferred_element_type=jnp.float32,
        )
        return scores + bias_ref[at, :]

    ahead = [score(*tile) for tile in tiles[:AHEAD]]
    for index, (g, s) in enumerate(tiles):
        if index + AHEAD < len(tiles):
            ahead.append(score(*tiles[index + AHEAD]))
        scores = ahead.pop(0)
        if s == 0:
            peaks, totals, outs = [], [], []
        peak = jnp.maximum(jnp.max(scores, 0, keepdims=True), SCORE_FLOOR * ROOT)
        weights = jnp.exp2((scores - peak) * TO_BITS)
        peaks.append(peak)
        totals.append(jnp.sum(weights, 0, keepdims=True))
        outs.append(
            jnp.dot(
                vt_ref[(first + g) * HD : (first + g + 1) * HD, s * segment : (s + 1) * segment],
                weights.astype(jnp.bfloat16),
                preferred_element_type=jnp.float32,
            )
        )
        if s < segments - 1:
            continue
        top = functools.reduce(jnp.maximum, peaks)
        scales = [jnp.exp2((peak - top) * TO_BITS) for peak in peaks]
        total = sum(e * t for e, t in zip(scales, totals))
        out = sum(e * o for e, o in zip(scales, outs))
        live = total > 0
        safe = jnp.where(live, total, 1.0)
        level = jnp.where(live, top * TO_BITS + jnp.log2(safe), NO_WEIGHT)
        out = out * jnp.where(live, 1.0 / safe, 0.0)
        largest = jnp.max(jnp.abs(out), 0, keepdims=True)
        power = jnp.clip(jnp.ceil(jnp.log2(jnp.maximum(largest, 1e-37))), -100.0, 8.0)
        out = jnp.round((out * (jnp.exp2(-power) * STEPS)).T).astype(jnp.int32).astype(jnp.int16)
        fixed = jnp.round(level * FIX).astype(jnp.int32)
        values = [fixed >> 16, (fixed & 0xFFFF) - 32768, power]
        for kind in range(KINDS):
            stats[kind][first + g] = values[kind].astype(jnp.float32)
        for h in range(GROUP):
            out_ref[:, (g * GROUP + h) * HD : (g * GROUP + h + 1) * HD] = out[h * rows : (h + 1) * rows]
    gap = jnp.zeros((SLOT - KV_SLOT, lanes), jnp.float32)
    high, low, power = [jnp.concatenate(kind, 0) for kind in stats]
    empty = jnp.zeros((KV_SLOT, lanes), jnp.float32)
    packed = []
    for upper, lower in ((high, low), (power, empty)):
        turned = jnp.concatenate([upper, gap, lower, gap], 0).T
        packed.append(
            sum(
                pltpu.roll(turned[h * rows : (h + 1) * rows], h * KV_SLOT, 1) if h else turned[:rows]
                for h in range(GROUP)
            )
        )
    packed = jnp.concatenate(packed, 1).astype(jnp.int32).astype(jnp.int16)
    out_ref[:, kv_heads * GROUP * HD :] = packed


def combine_kernel(*refs, layout, heads, final):
    wide = heads * HD
    sources = []
    for number in layout:
        sources.append(refs[:number])
        refs = refs[number:]
    out_refs = refs
    rows = sources[0][0].shape[0]
    chunk = rows // len(out_refs)
    fixed, powers = [], []
    for source in sources:
        stats = sum(ref[:, wide // len(source) :].astype(jnp.int32) for ref in source)
        level = stats[:, :HD]
        fixed.append((level << 16) + pltpu.roll(level, SLOT, 1) + 32768)
        powers.append(stats[:, HD:].astype(jnp.float32))
    top = functools.reduce(jnp.maximum, fixed)
    weights = [jnp.exp2((f - top).astype(jnp.float32) * (1.0 / FIX)) for f in fixed]
    total = sum(weights)
    shares = [w / total for w in weights]
    amounts = [s * jnp.exp2(p) for s, p in zip(shares, powers)]
    if final:
        factors = [a * (1.0 / STEPS) for a in amounts]
    else:
        power = jnp.clip(jnp.ceil(jnp.log2(jnp.maximum(sum(amounts), 1e-37))), -100.0, 8.0)
        back = jnp.exp2(-power)
        factors = [a * back for a in amounts]
    for h in range(heads):
        at = slice(h * HD, (h + 1) * HD)
        values = []
        for source in sources:
            share = heads // len(source)
            ref, local = source[h // share], h % share
            values.append(ref[:, local * HD : (local + 1) * HD].astype(jnp.int32))
        lane = h % GROUP * KV_SLOT + h // GROUP
        out = sum(f[:, lane : lane + 1] * v.astype(jnp.float32) for f, v in zip(factors, values))
        if final:
            out = out.astype(jnp.bfloat16)
        else:
            out = jnp.round(out).astype(jnp.int32).astype(jnp.int16)
        for c, out_ref in enumerate(out_refs):
            out_ref[:, at] = out[c * chunk : (c + 1) * chunk]
    if not final:
        level = top + jnp.round(jnp.log2(total) * FIX).astype(jnp.int32)
        lane = lax.broadcasted_iota(jnp.int32, level.shape, 1)
        low = pltpu.roll((level & 0xFFFF) - 32768, SLOT, 1)
        packed = jnp.concatenate(
            [jnp.where(lane < SLOT, level >> 16, low), power.astype(jnp.int32)], 1
        )
        packed = packed.astype(jnp.int16)
        for c, out_ref in enumerate(out_refs):
            out_ref[:, wide:] = packed[c * chunk : (c + 1) * chunk]


def combine(sources, pieces, heads, final):
    rows = sources[0][0].shape[0]
    width = heads * HD + (0 if final else STATS)
    dtype = jnp.bfloat16 if final else jnp.int16
    arrays = [array for source in sources for array in source]
    return pl.pallas_call(
        functools.partial(
            combine_kernel, layout=[len(source) for source in sources], heads=heads, final=final
        ),
        out_shape=[jax.ShapeDtypeStruct((rows // pieces, width), dtype)] * pieces,
        in_specs=[VMEM] * len(arrays),
        out_specs=[VMEM] * pieces,
        compiler_params=PARAMS,
    )(*arrays)


def fetch_kernel(in_ref, out_ref, sem):
    copy = pltpu.make_async_copy(in_ref, out_ref, sem)
    copy.start()
    copy.wait()


def fetch(array):
    return pl.pallas_call(
        fetch_kernel,
        out_shape=jax.ShapeDtypeStruct(array.shape, array.dtype),
        in_specs=[pl.BlockSpec(memory_space=pl.ANY)],
        out_specs=VMEM,
        scratch_shapes=[pltpu.SemaphoreType.DMA],
        compiler_params=PARAMS,
    )(array)


def on_device(queries, keys, values, block_live, span_offset):
    count = lax.axis_size("kv")
    q_dev, q_width = queries.shape
    kv_dev, kv_width = keys.shape
    heads = q_width // HD
    steps = exchange_steps(count)
    places = []
    for deltas in steps:
        places += [(deltas[1] << b).bit_length() - 1 for b in range(len(deltas).bit_length() - 1)]
    parts = len(steps[-1])
    chunk = count * q_dev // parts

    prepared = pl.pallas_call(
        functools.partial(prep_kernel, places=places),
        out_shape=[jax.ShapeDtypeStruct((kv_width, kv_dev), values.dtype)]
        + [jax.ShapeDtypeStruct((kv_dev, chunk * GROUP), jnp.float32)] * parts,
        in_specs=[VMEM] * 2 + [pl.BlockSpec(memory_space=pltpu.SMEM)],
        out_specs=[VMEM] * (1 + parts),
        compiler_params=PARAMS,
        cost_estimate=pl.CostEstimate(flops=0, bytes_accessed=4 * 2**20, transcendentals=0),
    )(values, block_live.T, span_offset)

    block = queries
    for stage, deltas in enumerate(steps[:-2]):
        others = [swap(block, d) for d in deltas[2:] + deltas[1:2]]
        if stage == 0:
            others, block = lax.optimization_barrier((others, fetch(block)))
        block = join([block] + others[-1:] + others[:-1])
    pieces = [block]
    for deltas in steps[-2:]:
        moved = [swap(p, d) for d in deltas[1:] for p in pieces]
        if deltas is steps[-2]:
            moved, prepared = lax.optimization_barrier((moved, prepared))
        pieces = pieces + moved
    v_turned, *biases = prepared

    def attend(pieces, bias, part, cuts):
        width = q_width // cuts
        return pl.pallas_call(
            functools.partial(
                attend_kernel, segment=kv_dev // 2, first=part * (heads // GROUP // cuts)
            ),
            out_shape=jax.ShapeDtypeStruct((chunk, width + STATS), jnp.int16),
            in_specs=[VMEM] * (len(pieces) + 3),
            out_specs=VMEM,
            compiler_params=PARAMS,
            cost_estimate=pl.CostEstimate(
                flops=4 * chunk * width * kv_dev,
                bytes_accessed=4 * 2**20 // cuts,
                transcendentals=chunk * width // HD * kv_dev,
            ),
        )(*pieces, keys, v_turned, bias)

    share = len(pieces) // parts
    early = attend(pieces[:share], biases[0], 0, 2)
    *others, early = lax.optimization_barrier((*pieces[share:], early))
    late = [
        attend(others[c * share : (c + 1) * share], biases[c + 1], 0, 1) for c in range(parts - 1)
    ]
    outs = [early] + late
    splits = [len(deltas) for deltas in steps[::-1]] + [1]
    for stage, deltas in enumerate(steps[::-1]):
        sources = [[swap(p, d)] for p, d in zip(outs[:0:-1], deltas[:0:-1])]
        own = [outs[0]]
        if stage == 0:
            own.append(attend(pieces[:share], biases[0], 1, 2))
            own[1], sources = lax.optimization_barrier((own[1], sources))
        outs = combine([own] + sources, splits[stage + 1], heads, stage == len(steps) - 1)
    return outs[0]


def solution(mesh):
    placed = (
        P(("groups", "kv"), None),
        P(("groups", "kv"), None),
        P(("groups", "kv"), None),
        P("groups", "kv"),
        P("groups"),
    )
    return jax.shard_map(
        on_device, mesh=mesh, in_specs=placed, out_specs=P(("groups", "kv"), None), check_vma=False
    )
```

```python
import functools
import math

import jax
import jax.numpy as jnp
from jax import lax
from jax.experimental import pallas as pl
from jax.experimental.pallas import tpu as pltpu
from jax.sharding import PartitionSpec as P

H = 64
KVH = 8
HD = 128
BLK = 64
GROUP = H // KVH
SCORE_FLOOR = -30.0
ROOT = math.sqrt(HD)
TO_BITS = math.log2(math.e) / ROOT
FIX = 2.0**17
STEPS = 32766.0
NO_WEIGHT = -8191.0
MASKED = -1e30
AHEAD = 1
KINDS = 3
SLOT = HD // 2
STATS = 2 * HD
KV_SLOT = SLOT // GROUP
VMEM = pl.BlockSpec(memory_space=pltpu.VMEM)
PARAMS = pltpu.CompilerParams(vmem_limit_bytes=24 * 2**20)


def swap(array, delta):
    count = lax.axis_size("kv")
    return lax.ppermute(array, "kv", [(i, i ^ delta) for i in range(count)])


def exchange_steps(count):
    bits = count.bit_length() - 1
    steps = []
    bit = 2
    while bit < bits:
        width = min(2, bits - bit)
        steps.append([d << bit for d in range(1 << width)])
        bit += width
    return steps[::-1]


def prep_kernel(v_ref, live_ref, offset_ref, v_turned, *bias_refs, places):
    me = lax.axis_index("kv")
    kv_dev = v_ref.shape[0]
    count = 2 ** len(places)
    lanes = bias_refs[0].shape[1]
    rows = lanes // GROUP
    q_dev = rows * len(bias_refs) // count
    offset = offset_ref[0]
    row = lax.broadcasted_iota(jnp.int32, (1, lanes), 1) % rows
    at_key = me * kv_dev + lax.broadcasted_iota(jnp.int32, (kv_dev, lanes), 0)
    live = live_ref[...].astype(jnp.float32)
    for c, bias_ref in enumerate(bias_refs):
        index = c * (count // len(bias_refs)) + row // q_dev
        owner = me
        for bit, place in enumerate(places):
            owner = owner ^ (((index >> bit) & 1) << place)
        token = owner * q_dev + row % q_dev
        chosen = lax.broadcasted_iota(jnp.int32, (count, lanes), 0) == owner
        seen = jnp.dot(live, chosen.astype(jnp.float32), preferred_element_type=jnp.float32)
        seen = jnp.concatenate(
            [jnp.broadcast_to(seen[b : b + 1], (BLK, lanes)) for b in range(kv_dev // BLK)], 0
        )
        allowed = (at_key <= offset + token) & ((at_key >= offset) | (seen > 0.5))
        bias_ref[...] = jnp.where(allowed, 0.0, MASKED)
    v_turned[...] = v_ref[...].T


def join_kernel(*refs):
    *in_refs, out_ref = refs
    joined = jnp.concatenate([ref[...].astype(jnp.float32) for ref in in_refs], 0)
    out_ref[...] = joined.astype(out_ref.dtype)


def join(pieces):
    rows, width = pieces[0].shape
    return pl.pallas_call(
        join_kernel,
        out_shape=jax.ShapeDtypeStruct((len(pieces) * rows, width), pieces[0].dtype),
        in_specs=[VMEM] * len(pieces),
        out_specs=VMEM,
        compiler_params=PARAMS,
    )(*pieces)


def attend_kernel(*refs, segment):
    q_refs, (k_ref, vt_ref, bias_ref), out_refs = refs[:2], refs[2:5], refs[5:]
    queries_all = jnp.concatenate([ref[...] for ref in q_refs], 0)
    rows, width = queries_all.shape
    chunk = rows // len(out_refs)
    kv_heads = width // (GROUP * HD)
    segments = k_ref.shape[0] // segment
    lanes = GROUP * rows
    stats = [[jnp.zeros((1, lanes), jnp.float32)] * KV_SLOT for _ in range(KINDS)]
    tiles = [(g, s) for g in range(kv_heads) for s in range(segments)]
    queries = {}

    def score(g, s):
        if g not in queries:
            queries[g] = jnp.concatenate(
                [
                    queries_all[:, (g * GROUP + h) * HD : (g * GROUP + h + 1) * HD]
                    for h in range(GROUP)
                ],
                0,
            )
        at = slice(s * segment, (s + 1) * segment)
        scores = lax.dot_general(
            k_ref[at, g * HD : (g + 1) * HD],
            queries[g],
            (((1,), (1,)), ((), ())),
            preferred_element_type=jnp.float32,
        )
        return scores + bias_ref[at, :]

    ahead = [score(*tile) for tile in tiles[:AHEAD]]
    for index, (g, s) in enumerate(tiles):
        if index + AHEAD < len(tiles):
            ahead.append(score(*tiles[index + AHEAD]))
        scores = ahead.pop(0)
        if s == 0:
            peaks, totals, outs = [], [], []
        peak = jnp.maximum(jnp.max(scores, 0, keepdims=True), SCORE_FLOOR * ROOT)
        weights = jnp.exp2((scores - peak) * TO_BITS)
        peaks.append(peak)
        totals.append(jnp.sum(weights, 0, keepdims=True))
        outs.append(
            jnp.dot(
                vt_ref[g * HD : (g + 1) * HD, s * segment : (s + 1) * segment],
                weights.astype(jnp.bfloat16),
                preferred_element_type=jnp.float32,
            )
        )
        if s < segments - 1:
            continue
        top = functools.reduce(jnp.maximum, peaks)
        scales = [jnp.exp2((peak - top) * TO_BITS) for peak in peaks]
        total = sum(e * t for e, t in zip(scales, totals))
        out = sum(e * o for e, o in zip(scales, outs))
        live = total > 0
        safe = jnp.where(live, total, 1.0)
        level = jnp.where(live, top * TO_BITS + jnp.log2(safe), NO_WEIGHT)
        out = out * jnp.where(live, 1.0 / safe, 0.0)
        largest = jnp.max(jnp.abs(out), 0, keepdims=True)
        power = jnp.clip(jnp.ceil(jnp.log2(jnp.maximum(largest, 1e-37))), -100.0, 8.0)
        out = jnp.round((out * (jnp.exp2(-power) * STEPS)).T).astype(jnp.int32)
        fixed = jnp.round(level * FIX).astype(jnp.int32)
        values = [fixed >> 16, (fixed & 0xFFFF) - 32768, power]
        for kind in range(KINDS):
            stats[kind][g] = values[kind].astype(jnp.float32)
        for h in range(GROUP):
            at = slice((g * GROUP + h) * HD, (g * GROUP + h + 1) * HD)
            for c, out_ref in enumerate(out_refs):
                top_row = h * rows + c * chunk
                out_ref[:, at] = out[top_row : top_row + chunk].astype(jnp.int16)
    gap = jnp.zeros((SLOT - KV_SLOT, lanes), jnp.float32)
    high, low, power = [jnp.concatenate(kind, 0) for kind in stats]
    empty = jnp.zeros((KV_SLOT, lanes), jnp.float32)
    packed = []
    for upper, lower in ((high, low), (power, empty)):
        turned = jnp.concatenate([upper, gap, lower, gap], 0).T
        packed.append(
            sum(
                pltpu.roll(turned[h * rows : (h + 1) * rows], h * KV_SLOT, 1) if h else turned[:rows]
                for h in range(GROUP)
            )
        )
    packed = jnp.concatenate(packed, 1).astype(jnp.int32)
    for c, out_ref in enumerate(out_refs):
        out_ref[:, width:] = packed[c * chunk : (c + 1) * chunk].astype(jnp.int16)


def combine_kernel(*refs, parts, heads, final):
    sources, out_refs = refs[:parts], refs[parts:]
    wide = heads * HD
    rows = sources[0].shape[0]
    chunk = rows // len(out_refs)
    fixed, powers = [], []
    for source in sources:
        stats = source[:, wide:].astype(jnp.int32)
        level = stats[:, :HD]
        fixed.append((level << 16) + pltpu.roll(level, SLOT, 1) + 32768)
        powers.append(stats[:, HD:].astype(jnp.float32))
    top = functools.reduce(jnp.maximum, fixed)
    weights = [jnp.exp2((f - top).astype(jnp.float32) * (1.0 / FIX)) for f in fixed]
    total = sum(weights)
    shares = [w / total for w in weights]
    amounts = [s * jnp.exp2(p) for s, p in zip(shares, powers)]
    if final:
        factors = [a * (1.0 / STEPS) for a in amounts]
    else:
        power = jnp.clip(jnp.ceil(jnp.log2(jnp.maximum(sum(amounts), 1e-37))), -100.0, 8.0)
        back = jnp.exp2(-power)
        factors = [a * back for a in amounts]
    for h in range(heads):
        at = slice(h * HD, (h + 1) * HD)
        at = slice(h * HD, (h + 1) * HD)
        values = [source[:, at].astype(jnp.int32) for source in sources]
        lane = h % GROUP * KV_SLOT + h // GROUP
        out = sum(f[:, lane : lane + 1] * v.astype(jnp.float32) for f, v in zip(factors, values))
        if final:
            out = out.astype(jnp.bfloat16)
        else:
            out = jnp.round(out).astype(jnp.int32).astype(jnp.int16)
        for c, out_ref in enumerate(out_refs):
            out_ref[:, at] = out[c * chunk : (c + 1) * chunk]
    if not final:
        level = top + jnp.round(jnp.log2(total) * FIX).astype(jnp.int32)
        lane = lax.broadcasted_iota(jnp.int32, level.shape, 1)
        low = pltpu.roll((level & 0xFFFF) - 32768, SLOT, 1)
        packed = jnp.concatenate(
            [jnp.where(lane < SLOT, level >> 16, low), power.astype(jnp.int32)], 1
        )
        packed = packed.astype(jnp.int16)
        for c, out_ref in enumerate(out_refs):
            out_ref[:, wide:] = packed[c * chunk : (c + 1) * chunk]


def combine(arrays, pieces, heads, final=False):
    rows = arrays[0].shape[0]
    width = heads * HD + (0 if final else STATS)
    dtype = jnp.bfloat16 if final else jnp.int16
    return pl.pallas_call(
        functools.partial(combine_kernel, parts=len(arrays), heads=heads, final=final),
        out_shape=[jax.ShapeDtypeStruct((rows // pieces, width), dtype)] * pieces,
        in_specs=[VMEM] * len(arrays),
        out_specs=[VMEM] * pieces,
        compiler_params=PARAMS,
    )(*arrays)


def fetch_kernel(in_ref, out_ref, sem):
    copy = pltpu.make_async_copy(in_ref, out_ref, sem)
    copy.start()
    copy.wait()


def fetch(array):
    return pl.pallas_call(
        fetch_kernel,
        out_shape=jax.ShapeDtypeStruct(array.shape, array.dtype),
        in_specs=[pl.BlockSpec(memory_space=pl.ANY)],
        out_specs=VMEM,
        scratch_shapes=[pltpu.SemaphoreType.DMA],
        compiler_params=PARAMS,
    )(array)


def on_device(queries, keys, values, block_live, span_offset):
    count = lax.axis_size("kv")
    q_dev, q_width = queries.shape
    kv_dev, kv_width = keys.shape
    heads = q_width // HD
    steps = exchange_steps(count)
    places = []
    for deltas in steps:
        places += [(deltas[1] << b).bit_length() - 1 for b in range(len(deltas).bit_length() - 1)]
    places += [0, 1]
    parts = 2
    chunk = count * q_dev // parts

    prepared = pl.pallas_call(
        functools.partial(prep_kernel, places=places),
        out_shape=[jax.ShapeDtypeStruct((kv_width, kv_dev), values.dtype)]
        + [jax.ShapeDtypeStruct((kv_dev, chunk * GROUP), jnp.float32)] * parts,
        in_specs=[VMEM] * 2 + [pl.BlockSpec(memory_space=pltpu.SMEM)],
        out_specs=[VMEM] * (1 + parts),
        compiler_params=PARAMS,
        cost_estimate=pl.CostEstimate(flops=0, bytes_accessed=4 * 2**20, transcendentals=0),
    )(values, block_live.T, span_offset)

    block = queries
    for stage, deltas in enumerate(steps):
        others = [swap(block, d) for d in deltas[:0:-1]]
        if stage == 0:
            others, block = lax.optimization_barrier((others, fetch(block)))
        block = join([block] + others[::-1])
    v_turned, near_bias, far_bias = prepared

    def attend(pair, bias):
        return pl.pallas_call(
            functools.partial(attend_kernel, segment=kv_dev // 2),
            out_shape=[jax.ShapeDtypeStruct((chunk // 2, q_width + STATS), jnp.int16)] * 2,
            in_specs=[VMEM] * 5,
            out_specs=[VMEM] * 2,
            compiler_params=PARAMS,
            cost_estimate=pl.CostEstimate(
                flops=4 * chunk * q_width * kv_dev,
                bytes_accessed=4 * 2**20,
                transcendentals=chunk * heads * kv_dev,
            ),
        )(*pair, keys, v_turned, bias)

    far_block = swap(block, 2)
    near = attend([block, swap(block, 1)], near_bias)
    far_block, near = lax.optimization_barrier((far_block, near))
    far = attend([far_block, swap(far_block, 1)], far_bias)
    (far_sum,) = combine([far[0], swap(far[1], 1)], 1, heads)
    (near_sum,) = combine([near[0], swap(near[1], 1)], 1, heads)
    arrays = [near_sum, swap(far_sum, 2)]
    for deltas in steps[::-1]:
        outs = combine(arrays, len(deltas), heads)
        sent = [swap(p, d) for p, d in zip(outs[1:], deltas[1:])]
        arrays = [outs[0]] + sent[:1] + sent[:0:-1]
    return combine(arrays, 1, heads, final=True)[0]


def solution(mesh):
    placed = (
        P(("groups", "kv"), None),
        P(("groups", "kv"), None),
        P(("groups", "kv"), None),
        P("groups", "kv"),
        P("groups"),
    )
    return jax.shard_map(
        on_device, mesh=mesh, in_specs=placed, out_specs=P(("groups", "kv"), None), check_vma=False
    )
```

```python
import functools
import math

import jax
import jax.numpy as jnp
from jax import lax
from jax.experimental import pallas as pl
from jax.experimental.pallas import tpu as pltpu
from jax.sharding import PartitionSpec as P

H = 64
KVH = 8
HD = 128
BLK = 64
GROUP = H // KVH
SCORE_FLOOR = -30.0
ROOT = math.sqrt(HD)
TO_BITS = math.log2(math.e) / ROOT
FIX = 2.0**17
STEPS = 32766.0
NO_WEIGHT = -8191.0
MASKED = -1e30
AHEAD = 1
KINDS = 3
SLOT = HD // 2
STATS = 2 * HD
KV_SLOT = SLOT // GROUP
VMEM = pl.BlockSpec(memory_space=pltpu.VMEM)
PARAMS = pltpu.CompilerParams(vmem_limit_bytes=24 * 2**20)


def swap(array, delta):
    count = lax.axis_size("kv")
    return lax.ppermute(array, "kv", [(i, i ^ delta) for i in range(count)])


def exchange_steps(count):
    bits = count.bit_length() - 1
    steps = []
    bit = 2
    while bit < bits:
        width = min(2, bits - bit)
        steps.append([d << bit for d in range(1 << width)])
        bit += width
    return steps[::-1]


def prep_kernel(v_ref, live_ref, offset_ref, v_turned, *bias_refs, places):
    me = lax.axis_index("kv")
    kv_dev = v_ref.shape[0]
    count = 2 ** len(places)
    lanes = bias_refs[0].shape[1]
    rows = lanes // GROUP
    q_dev = rows * len(bias_refs) // count
    offset = offset_ref[0]
    row = lax.broadcasted_iota(jnp.int32, (1, lanes), 1) % rows
    at_key = me * kv_dev + lax.broadcasted_iota(jnp.int32, (kv_dev, lanes), 0)
    live = live_ref[...].astype(jnp.float32)
    for c, bias_ref in enumerate(bias_refs):
        index = c * (count // len(bias_refs)) + row // q_dev
        owner = me
        for bit, place in enumerate(places):
            owner = owner ^ (((index >> bit) & 1) << place)
        token = owner * q_dev + row % q_dev
        chosen = lax.broadcasted_iota(jnp.int32, (count, lanes), 0) == owner
        seen = jnp.dot(live, chosen.astype(jnp.float32), preferred_element_type=jnp.float32)
        seen = jnp.concatenate(
            [jnp.broadcast_to(seen[b : b + 1], (BLK, lanes)) for b in range(kv_dev // BLK)], 0
        )
        allowed = (at_key <= offset + token) & ((at_key >= offset) | (seen > 0.5))
        bias_ref[...] = jnp.where(allowed, 0.0, MASKED)
    v_turned[...] = v_ref[...].T


def join_kernel(*refs):
    *in_refs, out_ref = refs
    joined = jnp.concatenate([ref[...].astype(jnp.float32) for ref in in_refs], 0)
    out_ref[...] = joined.astype(out_ref.dtype)


def join(pieces):
    rows, width = pieces[0].shape
    return pl.pallas_call(
        join_kernel,
        out_shape=jax.ShapeDtypeStruct((len(pieces) * rows, width), pieces[0].dtype),
        in_specs=[VMEM] * len(pieces),
        out_specs=VMEM,
        compiler_params=PARAMS,
    )(*pieces)


def attend_kernel(*refs, segment, first):
    q_refs, (k_ref, vt_ref, bias_ref), out_refs = refs[:-5], refs[-5:-2], refs[-2:]
    width = out_refs[0].shape[1] - STATS
    start = first * GROUP * HD
    queries_all = jnp.concatenate([ref[:, start : start + width] for ref in q_refs], 0)
    rows = queries_all.shape[0]
    chunk = rows // len(out_refs)
    kv_heads = width // (GROUP * HD)
    segments = k_ref.shape[0] // segment
    lanes = GROUP * rows
    stats = [[jnp.zeros((1, lanes), jnp.float32)] * KV_SLOT for _ in range(KINDS)]
    tiles = [(g, s) for g in range(kv_heads) for s in range(segments)]
    queries = {}

    def score(g, s):
        if g not in queries:
            queries[g] = jnp.concatenate(
                [
                    queries_all[:, (g * GROUP + h) * HD : (g * GROUP + h + 1) * HD]
                    for h in range(GROUP)
                ],
                0,
            )
        at = slice(s * segment, (s + 1) * segment)
        scores = lax.dot_general(
            k_ref[at, (first + g) * HD : (first + g + 1) * HD],
            queries[g],
            (((1,), (1,)), ((), ())),
            preferred_element_type=jnp.float32,
        )
        return scores + bias_ref[at, :]

    ahead = [score(*tile) for tile in tiles[:AHEAD]]
    for index, (g, s) in enumerate(tiles):
        if index + AHEAD < len(tiles):
            ahead.append(score(*tiles[index + AHEAD]))
        scores = ahead.pop(0)
        if s == 0:
            peaks, totals, outs = [], [], []
        peak = jnp.maximum(jnp.max(scores, 0, keepdims=True), SCORE_FLOOR * ROOT)
        weights = jnp.exp2((scores - peak) * TO_BITS)
        peaks.append(peak)
        totals.append(jnp.sum(weights, 0, keepdims=True))
        outs.append(
            jnp.dot(
                vt_ref[(first + g) * HD : (first + g + 1) * HD, s * segment : (s + 1) * segment],
                weights.astype(jnp.bfloat16),
                preferred_element_type=jnp.float32,
            )
        )
        if s < segments - 1:
            continue
        top = functools.reduce(jnp.maximum, peaks)
        scales = [jnp.exp2((peak - top) * TO_BITS) for peak in peaks]
        total = sum(e * t for e, t in zip(scales, totals))
        out = sum(e * o for e, o in zip(scales, outs))
        live = total > 0
        safe = jnp.where(live, total, 1.0)
        level = jnp.where(live, top * TO_BITS + jnp.log2(safe), NO_WEIGHT)
        out = out * jnp.where(live, 1.0 / safe, 0.0)
        largest = jnp.max(jnp.abs(out), 0, keepdims=True)
        power = jnp.clip(jnp.ceil(jnp.log2(jnp.maximum(largest, 1e-37))), -100.0, 8.0)
        out = jnp.round((out * (jnp.exp2(-power) * STEPS)).T).astype(jnp.int32)
        fixed = jnp.round(level * FIX).astype(jnp.int32)
        values = [fixed >> 16, (fixed & 0xFFFF) - 32768, power]
        for kind in range(KINDS):
            stats[kind][first + g] = values[kind].astype(jnp.float32)
        for h in range(GROUP):
            at = slice((g * GROUP + h) * HD, (g * GROUP + h + 1) * HD)
            for c, out_ref in enumerate(out_refs):
                top_row = h * rows + c * chunk
                out_ref[:, at] = out[top_row : top_row + chunk].astype(jnp.int16)
    gap = jnp.zeros((SLOT - KV_SLOT, lanes), jnp.float32)
    high, low, power = [jnp.concatenate(kind, 0) for kind in stats]
    empty = jnp.zeros((KV_SLOT, lanes), jnp.float32)
    packed = []
    for upper, lower in ((high, low), (power, empty)):
        turned = jnp.concatenate([upper, gap, lower, gap], 0).T
        packed.append(
            sum(
                pltpu.roll(turned[h * rows : (h + 1) * rows], h * KV_SLOT, 1) if h else turned[:rows]
                for h in range(GROUP)
            )
        )
    packed = jnp.concatenate(packed, 1).astype(jnp.int32)
    for c, out_ref in enumerate(out_refs):
        out_ref[:, width:] = packed[c * chunk : (c + 1) * chunk].astype(jnp.int16)


def combine_kernel(*refs, layout, heads, final):
    wide = heads * HD
    sources = []
    for number in layout:
        sources.append(refs[:number])
        refs = refs[number:]
    out_refs = refs
    rows = sources[0][0].shape[0]
    chunk = rows // len(out_refs)
    fixed, powers = [], []
    for source in sources:
        stats = sum(ref[:, wide // len(source) :].astype(jnp.int32) for ref in source)
        level = stats[:, :HD]
        fixed.append((level << 16) + pltpu.roll(level, SLOT, 1) + 32768)
        powers.append(stats[:, HD:].astype(jnp.float32))
    top = functools.reduce(jnp.maximum, fixed)
    weights = [jnp.exp2((f - top).astype(jnp.float32) * (1.0 / FIX)) for f in fixed]
    total = sum(weights)
    shares = [w / total for w in weights]
    amounts = [s * jnp.exp2(p) for s, p in zip(shares, powers)]
    if final:
        factors = [a * (1.0 / STEPS) for a in amounts]
    else:
        power = jnp.clip(jnp.ceil(jnp.log2(jnp.maximum(sum(amounts), 1e-37))), -100.0, 8.0)
        back = jnp.exp2(-power)
        factors = [a * back for a in amounts]
    for h in range(heads):
        at = slice(h * HD, (h + 1) * HD)
        values = []
        for source in sources:
            share = heads // len(source)
            ref, local = source[h // share], h % share
            values.append(ref[:, local * HD : (local + 1) * HD].astype(jnp.int32))
        lane = h % GROUP * KV_SLOT + h // GROUP
        out = sum(f[:, lane : lane + 1] * v.astype(jnp.float32) for f, v in zip(factors, values))
        if final:
            out = out.astype(jnp.bfloat16)
        else:
            out = jnp.round(out).astype(jnp.int32).astype(jnp.int16)
        for c, out_ref in enumerate(out_refs):
            out_ref[:, at] = out[c * chunk : (c + 1) * chunk]
    if not final:
        level = top + jnp.round(jnp.log2(total) * FIX).astype(jnp.int32)
        lane = lax.broadcasted_iota(jnp.int32, level.shape, 1)
        low = pltpu.roll((level & 0xFFFF) - 32768, SLOT, 1)
        packed = jnp.concatenate(
            [jnp.where(lane < SLOT, level >> 16, low), power.astype(jnp.int32)], 1
        )
        packed = packed.astype(jnp.int16)
        for c, out_ref in enumerate(out_refs):
            out_ref[:, wide:] = packed[c * chunk : (c + 1) * chunk]


def combine(sources, pieces, heads, final=False):
    rows = sources[0][0].shape[0]
    width = heads * HD + (0 if final else STATS)
    dtype = jnp.bfloat16 if final else jnp.int16
    arrays = [array for source in sources for array in source]
    return pl.pallas_call(
        functools.partial(
            combine_kernel, layout=[len(source) for source in sources], heads=heads, final=final
        ),
        out_shape=[jax.ShapeDtypeStruct((rows // pieces, width), dtype)] * pieces,
        in_specs=[VMEM] * len(arrays),
        out_specs=[VMEM] * pieces,
        compiler_params=PARAMS,
    )(*arrays)


def fetch_kernel(in_ref, out_ref, sem):
    copy = pltpu.make_async_copy(in_ref, out_ref, sem)
    copy.start()
    copy.wait()


def fetch(array):
    return pl.pallas_call(
        fetch_kernel,
        out_shape=jax.ShapeDtypeStruct(array.shape, array.dtype),
        in_specs=[pl.BlockSpec(memory_space=pl.ANY)],
        out_specs=VMEM,
        scratch_shapes=[pltpu.SemaphoreType.DMA],
        compiler_params=PARAMS,
    )(array)


def on_device(queries, keys, values, block_live, span_offset):
    count = lax.axis_size("kv")
    q_dev, q_width = queries.shape
    kv_dev, kv_width = keys.shape
    heads = q_width // HD
    steps = exchange_steps(count)
    places = []
    for deltas in steps:
        places += [(deltas[1] << b).bit_length() - 1 for b in range(len(deltas).bit_length() - 1)]
    places += [1, 0]
    parts = 2
    chunk = count * q_dev // parts

    prepared = pl.pallas_call(
        functools.partial(prep_kernel, places=places),
        out_shape=[jax.ShapeDtypeStruct((kv_width, kv_dev), values.dtype)]
        + [jax.ShapeDtypeStruct((kv_dev, chunk * GROUP), jnp.float32)] * parts,
        in_specs=[VMEM] * 2 + [pl.BlockSpec(memory_space=pltpu.SMEM)],
        out_specs=[VMEM] * (1 + parts),
        compiler_params=PARAMS,
        cost_estimate=pl.CostEstimate(flops=0, bytes_accessed=4 * 2**20, transcendentals=0),
    )(values, block_live.T, span_offset)

    block = queries
    for stage, deltas in enumerate(steps):
        others = [swap(block, d) for d in deltas[2:] + deltas[1:2]]
        if stage == 0:
            others, block = lax.optimization_barrier((others, fetch(block)))
        block = join([block] + others[-1:] + others[:-1])
    far_block, prepared = lax.optimization_barrier((swap(block, 2), prepared))
    v_turned, own_bias, other_bias = prepared

    def attend(pair, bias, part, cuts):
        width = q_width // cuts
        return pl.pallas_call(
            functools.partial(
                attend_kernel, segment=kv_dev // 2, first=part * (heads // GROUP // cuts)
            ),
            out_shape=[jax.ShapeDtypeStruct((chunk // 2, width + STATS), jnp.int16)] * 2,
            in_specs=[VMEM] * 5,
            out_specs=[VMEM] * 2,
            compiler_params=PARAMS,
            cost_estimate=pl.CostEstimate(
                flops=4 * chunk * width * kv_dev,
                bytes_accessed=4 * 2**20 // cuts,
                transcendentals=chunk * width // HD * kv_dev,
            ),
        )(*pair, keys, v_turned, bias)

    pair, other_pair = [block, far_block], [swap(block, 1), swap(far_block, 1)]
    early = attend(pair, own_bias, 0, 2)
    other_pair, early = lax.optimization_barrier((other_pair, early))
    near, far = attend(other_pair, other_bias, 0, 1)
    late = attend(pair, own_bias, 1, 2)
    late, far = lax.optimization_barrier((late, swap(far, 1)))
    (far_sum,) = combine([[early[1], late[1]], [far]], 1, heads)
    (near_sum,) = combine([[early[0], late[0]], [swap(near, 1)]], 1, heads)
    arrays = [near_sum, swap(far_sum, 2)]
    for deltas in steps[::-1]:
        outs = combine([[a] for a in arrays], len(deltas), heads)
        sent = [swap(p, d) for p, d in zip(outs[1:], deltas[1:])]
        arrays = [outs[0]] + sent[::-1]
    return combine([[a] for a in arrays], 1, heads, final=True)[0]


def solution(mesh):
    placed = (
        P(("groups", "kv"), None),
        P(("groups", "kv"), None),
        P(("groups", "kv"), None),
        P("groups", "kv"),
        P("groups"),
    )
    return jax.shard_map(
        on_device, mesh=mesh, in_specs=placed, out_specs=P(("groups", "kv"), None), check_vma=False
    )
```

```python
import functools
import math

import jax
import jax.numpy as jnp
from jax import lax
from jax.experimental import pallas as pl
from jax.experimental.pallas import tpu as pltpu
from jax.sharding import PartitionSpec as P

H = 64
KVH = 8
HD = 128
BLK = 64
GROUP = H // KVH
SCORE_FLOOR = -30.0
ROOT = math.sqrt(HD)
TO_BITS = math.log2(math.e) / ROOT
FIX = 2.0**17
STEPS = 32766.0
NO_WEIGHT = -8191.0
MASKED = -1e30
AHEAD = 1
WRITES = 4
KINDS = 3
SLOT = HD // 2
STATS = 2 * HD
KV_SLOT = SLOT // GROUP
VMEM = pl.BlockSpec(memory_space=pltpu.VMEM)
PARAMS = pltpu.CompilerParams(vmem_limit_bytes=24 * 2**20)


def swap(array, delta):
    count = lax.axis_size("kv")
    return lax.ppermute(array, "kv", [(i, i ^ delta) for i in range(count)])


def exchange_steps(count):
    bits = count.bit_length() - 1
    steps = []
    bit = 2
    while bit < bits:
        width = min(2, bits - bit)
        steps.append([d << bit for d in range(1 << width)])
        bit += width
    return steps[::-1]


def prep_kernel(v_ref, live_ref, offset_ref, v_turned, *bias_refs, places):
    me = lax.axis_index("kv")
    kv_dev = v_ref.shape[0]
    count = 2 ** len(places)
    lanes = bias_refs[0].shape[1]
    rows = lanes // GROUP
    q_dev = rows * len(bias_refs) // count
    offset = offset_ref[0]
    row = lax.broadcasted_iota(jnp.int32, (1, lanes), 1) % rows
    at_key = me * kv_dev + lax.broadcasted_iota(jnp.int32, (kv_dev, lanes), 0)
    live = live_ref[...].astype(jnp.float32)
    for c, bias_ref in enumerate(bias_refs):
        index = c * (count // len(bias_refs)) + row // q_dev
        owner = me
        for bit, place in enumerate(places):
            owner = owner ^ (((index >> bit) & 1) << place)
        token = owner * q_dev + row % q_dev
        chosen = lax.broadcasted_iota(jnp.int32, (count, lanes), 0) == owner
        seen = jnp.dot(live, chosen.astype(jnp.float32), preferred_element_type=jnp.float32)
        seen = jnp.concatenate(
            [jnp.broadcast_to(seen[b : b + 1], (BLK, lanes)) for b in range(kv_dev // BLK)], 0
        )
        allowed = (at_key <= offset + token) & ((at_key >= offset) | (seen > 0.5))
        bias_ref[...] = jnp.where(allowed, 0.0, MASKED)
    v_turned[...] = v_ref[...].T


def join_kernel(*refs):
    *in_refs, out_ref = refs
    joined = jnp.concatenate([ref[...].astype(jnp.float32) for ref in in_refs], 0)
    out_ref[...] = joined.astype(out_ref.dtype)


def join(pieces):
    rows, width = pieces[0].shape
    return pl.pallas_call(
        join_kernel,
        out_shape=jax.ShapeDtypeStruct((len(pieces) * rows, width), pieces[0].dtype),
        in_specs=[VMEM] * len(pieces),
        out_specs=VMEM,
        compiler_params=PARAMS,
    )(*pieces)


def attend_kernel(*refs, segment, first):
    q_refs, (k_ref, vt_ref, bias_ref), out_refs = refs[:-5], refs[-5:-2], refs[-2:]
    width = out_refs[0].shape[1] - STATS
    start = first * GROUP * HD
    queries_all = jnp.concatenate([ref[:, start : start + width] for ref in q_refs], 0)
    rows = queries_all.shape[0]
    chunk = rows // len(out_refs)
    kv_heads = width // (GROUP * HD)
    segments = k_ref.shape[0] // segment
    lanes = GROUP * rows
    stats = [[jnp.zeros((1, lanes), jnp.float32)] * KV_SLOT for _ in range(KINDS)]
    tiles = [(g, s) for g in range(kv_heads) for s in range(segments)]
    queries = {}

    def score(g, s):
        if g not in queries:
            queries[g] = jnp.concatenate(
                [
                    queries_all[:, (g * GROUP + h) * HD : (g * GROUP + h + 1) * HD]
                    for h in range(GROUP)
                ],
                0,
            )
        at = slice(s * segment, (s + 1) * segment)
        scores = lax.dot_general(
            k_ref[at, (first + g) * HD : (first + g + 1) * HD],
            queries[g],
            (((1,), (1,)), ((), ())),
            preferred_element_type=jnp.float32,
        )
        return scores + bias_ref[at, :]

    ahead = [score(*tile) for tile in tiles[:AHEAD]]
    for index, (g, s) in enumerate(tiles):
        if index + AHEAD < len(tiles):
            ahead.append(score(*tiles[index + AHEAD]))
        scores = ahead.pop(0)
        if s == 0:
            peaks, totals, outs = [], [], []
        peak = jnp.maximum(jnp.max(scores, 0, keepdims=True), SCORE_FLOOR * ROOT)
        weights = jnp.exp2((scores - peak) * TO_BITS)
        peaks.append(peak)
        totals.append(jnp.sum(weights, 0, keepdims=True))
        outs.append(
            jnp.dot(
                vt_ref[(first + g) * HD : (first + g + 1) * HD, s * segment : (s + 1) * segment],
                weights.astype(jnp.bfloat16),
                preferred_element_type=jnp.float32,
            )
        )
        if s < segments - 1:
            continue
        top = functools.reduce(jnp.maximum, peaks)
        scales = [jnp.exp2((peak - top) * TO_BITS) for peak in peaks]
        total = sum(e * t for e, t in zip(scales, totals))
        out = sum(e * o for e, o in zip(scales, outs))
        live = total > 0
        safe = jnp.where(live, total, 1.0)
        level = jnp.where(live, top * TO_BITS + jnp.log2(safe), NO_WEIGHT)
        out = out * jnp.where(live, 1.0 / safe, 0.0)
        largest = jnp.max(jnp.abs(out), 0, keepdims=True)
        power = jnp.clip(jnp.ceil(jnp.log2(jnp.maximum(largest, 1e-37))), -100.0, 8.0)
        out = jnp.round((out * (jnp.exp2(-power) * STEPS)).T).astype(jnp.int32)
        fixed = jnp.round(level * FIX).astype(jnp.int32)
        values = [fixed >> 16, (fixed & 0xFFFF) - 32768, power]
        for kind in range(KINDS):
            stats[kind][first + g] = values[kind].astype(jnp.float32)
        for h in range(GROUP):
            at = slice((g * GROUP + h) * HD, (g * GROUP + h + 1) * HD)
            for c, out_ref in enumerate(out_refs):
                top_row = h * rows + c * chunk
                out_ref[:, at] = out[top_row : top_row + chunk].astype(jnp.int16)
    gap = jnp.zeros((SLOT - KV_SLOT, lanes), jnp.float32)
    high, low, power = [jnp.concatenate(kind, 0) for kind in stats]
    empty = jnp.zeros((KV_SLOT, lanes), jnp.float32)
    packed = []
    for upper, lower in ((high, low), (power, empty)):
        turned = jnp.concatenate([upper, gap, lower, gap], 0).T
        packed.append(
            sum(
                pltpu.roll(turned[h * rows : (h + 1) * rows], h * KV_SLOT, 1) if h else turned[:rows]
                for h in range(GROUP)
            )
        )
    packed = jnp.concatenate(packed, 1).astype(jnp.int32)
    for c, out_ref in enumerate(out_refs):
        out_ref[:, width:] = packed[c * chunk : (c + 1) * chunk].astype(jnp.int16)


def combine_kernel(*refs, layout, heads, final):
    wide = heads * HD
    sources = []
    for number in layout:
        sources.append(refs[:number])
        refs = refs[number:]
    out_refs = refs
    copies = []
    if final:
        target, stage, sems = refs
        out_refs = [stage]
    rows = sources[0][0].shape[0]
    chunk = rows // len(out_refs)
    fixed, powers = [], []
    for source in sources:
        stats = sum(ref[:, wide // len(source) :].astype(jnp.int32) for ref in source)
        level = stats[:, :HD]
        fixed.append((level << 16) + pltpu.roll(level, SLOT, 1) + 32768)
        powers.append(stats[:, HD:].astype(jnp.float32))
    top = functools.reduce(jnp.maximum, fixed)
    weights = [jnp.exp2((f - top).astype(jnp.float32) * (1.0 / FIX)) for f in fixed]
    total = sum(weights)
    shares = [w / total for w in weights]
    amounts = [s * jnp.exp2(p) for s, p in zip(shares, powers)]
    if final:
        factors = [a * (1.0 / STEPS) for a in amounts]
    else:
        power = jnp.clip(jnp.ceil(jnp.log2(jnp.maximum(sum(amounts), 1e-37))), -100.0, 8.0)
        back = jnp.exp2(-power)
        factors = [a * back for a in amounts]
    for h in range(heads):
        at = slice(h * HD, (h + 1) * HD)
        values = []
        for source in sources:
            share = heads // len(source)
            ref, local = source[h // share], h % share
            values.append(ref[:, local * HD : (local + 1) * HD].astype(jnp.int32))
        lane = h % GROUP * KV_SLOT + h // GROUP
        out = sum(f[:, lane : lane + 1] * v.astype(jnp.float32) for f, v in zip(factors, values))
        if final:
            out = out.astype(jnp.bfloat16)
        else:
            out = jnp.round(out).astype(jnp.int32).astype(jnp.int16)
        for c, out_ref in enumerate(out_refs):
            out_ref[:, at] = out[c * chunk : (c + 1) * chunk]
        if final and (h + 1) % (heads // WRITES) == 0:
            piece = wide // WRITES
            done = pl.ds(len(copies) * piece, piece)
            copies.append(
                pltpu.make_async_copy(stage.at[:, done], target.at[:, done], sems.at[len(copies)])
            )
            copies[-1].start()
    for copy in copies:
        copy.wait()
    if not final:
        level = top + jnp.round(jnp.log2(total) * FIX).astype(jnp.int32)
        lane = lax.broadcasted_iota(jnp.int32, level.shape, 1)
        low = pltpu.roll((level & 0xFFFF) - 32768, SLOT, 1)
        packed = jnp.concatenate(
            [jnp.where(lane < SLOT, level >> 16, low), power.astype(jnp.int32)], 1
        )
        packed = packed.astype(jnp.int16)
        for c, out_ref in enumerate(out_refs):
            out_ref[:, wide:] = packed[c * chunk : (c + 1) * chunk]


def combine(sources, pieces, heads, final=False):
    rows = sources[0][0].shape[0]
    width = heads * HD + (0 if final else STATS)
    dtype = jnp.bfloat16 if final else jnp.int16
    arrays = [array for source in sources for array in source]
    return pl.pallas_call(
        functools.partial(
            combine_kernel, layout=[len(source) for source in sources], heads=heads, final=final
        ),
        out_shape=[jax.ShapeDtypeStruct((rows // pieces, width), dtype)] * pieces,
        in_specs=[VMEM] * len(arrays),
        out_specs=[pl.BlockSpec(memory_space=pl.ANY) if final else VMEM] * pieces,
        scratch_shapes=[pltpu.VMEM((rows, width), dtype), pltpu.SemaphoreType.DMA((WRITES,))]
        if final
        else [],
        compiler_params=PARAMS,
    )(*arrays)


def fetch_kernel(in_ref, out_ref, sem):
    copy = pltpu.make_async_copy(in_ref, out_ref, sem)
    copy.start()
    copy.wait()


def fetch(array):
    return pl.pallas_call(
        fetch_kernel,
        out_shape=jax.ShapeDtypeStruct(array.shape, array.dtype),
        in_specs=[pl.BlockSpec(memory_space=pl.ANY)],
        out_specs=VMEM,
        scratch_shapes=[pltpu.SemaphoreType.DMA],
        compiler_params=PARAMS,
    )(array)


def on_device(queries, keys, values, block_live, span_offset):
    count = lax.axis_size("kv")
    q_dev, q_width = queries.shape
    kv_dev, kv_width = keys.shape
    heads = q_width // HD
    steps = exchange_steps(count)
    places = []
    for deltas in steps:
        places += [(deltas[1] << b).bit_length() - 1 for b in range(len(deltas).bit_length() - 1)]
    places += [1, 0]
    parts = 2
    chunk = count * q_dev // parts

    prepared = pl.pallas_call(
        functools.partial(prep_kernel, places=places),
        out_shape=[jax.ShapeDtypeStruct((kv_width, kv_dev), values.dtype)]
        + [jax.ShapeDtypeStruct((kv_dev, chunk * GROUP), jnp.float32)] * parts,
        in_specs=[VMEM] * 2 + [pl.BlockSpec(memory_space=pltpu.SMEM)],
        out_specs=[VMEM] * (1 + parts),
        compiler_params=PARAMS,
        cost_estimate=pl.CostEstimate(flops=0, bytes_accessed=4 * 2**20, transcendentals=0),
    )(values, block_live.T, span_offset)

    block = queries
    for stage, deltas in enumerate(steps):
        others = [swap(block, d) for d in deltas[2:] + deltas[1:2]]
        if stage == 0:
            others, block = lax.optimization_barrier((others, fetch(block)))
        block = join([block] + others[-1:] + others[:-1])
    far_block, prepared = lax.optimization_barrier((swap(block, 2), prepared))
    v_turned, own_bias, other_bias = prepared

    def attend(pair, bias, part, cuts):
        width = q_width // cuts
        return pl.pallas_call(
            functools.partial(
                attend_kernel, segment=kv_dev // 2, first=part * (heads // GROUP // cuts)
            ),
            out_shape=[jax.ShapeDtypeStruct((chunk // 2, width + STATS), jnp.int16)] * 2,
            in_specs=[VMEM] * 5,
            out_specs=[VMEM] * 2,
            compiler_params=PARAMS,
            cost_estimate=pl.CostEstimate(
                flops=4 * chunk * width * kv_dev,
                bytes_accessed=4 * 2**20 // cuts,
                transcendentals=chunk * width // HD * kv_dev,
            ),
        )(*pair, keys, v_turned, bias)

    pair, other_pair = [block, far_block], [swap(block, 1), swap(far_block, 1)]
    early = attend(pair, own_bias, 0, 2)
    other_pair, early = lax.optimization_barrier((other_pair, early))
    near, far = attend(other_pair, other_bias, 0, 1)
    late = attend(pair, own_bias, 1, 2)
    late, far = lax.optimization_barrier((late, swap(far, 1)))
    (far_sum,) = combine([[early[1], late[1]], [far]], 1, heads)
    (near_sum,) = combine([[early[0], late[0]], [swap(near, 1)]], 1, heads)
    arrays = [near_sum, swap(far_sum, 2)]
    for deltas in steps[::-1]:
        outs = combine([[a] for a in arrays], len(deltas), heads)
        sent = [swap(p, d) for p, d in zip(outs[1:], deltas[1:])]
        arrays = [outs[0]] + sent[::-1]
    return combine([[a] for a in arrays], 1, heads, final=True)[0]


def solution(mesh):
    placed = (
        P(("groups", "kv"), None),
        P(("groups", "kv"), None),
        P(("groups", "kv"), None),
        P("groups", "kv"),
        P("groups"),
    )
    return jax.shard_map(
        on_device, mesh=mesh, in_specs=placed, out_specs=P(("groups", "kv"), None), check_vma=False
    )
```

```python
import functools
import math

import jax
import jax.numpy as jnp
from jax import lax
from jax.experimental import pallas as pl
from jax.experimental.pallas import tpu as pltpu
from jax.sharding import PartitionSpec as P

H = 64
KVH = 8
HD = 128
BLK = 64
GROUP = H // KVH
SCORE_FLOOR = -30.0
ROOT = math.sqrt(HD)
TO_BITS = math.log2(math.e) / ROOT
FIX = 2.0**17
STEPS = 32766.0
NO_WEIGHT = -8191.0
MASKED = -1e30
AHEAD = 2
WRITES = 4
KINDS = 3
SLOT = HD // 2
STATS = 2 * HD
KV_SLOT = SLOT // GROUP
VMEM = pl.BlockSpec(memory_space=pltpu.VMEM)
PARAMS = pltpu.CompilerParams(vmem_limit_bytes=24 * 2**20)


def swap(array, delta):
    count = lax.axis_size("kv")
    return lax.ppermute(array, "kv", [(i, i ^ delta) for i in range(count)])


def exchange_steps(count):
    bits = count.bit_length() - 1
    steps = []
    bit = 2
    while bit < bits:
        width = min(2, bits - bit)
        steps.append([d << bit for d in range(1 << width)])
        bit += width
    return steps[::-1]


def prep_kernel(v_ref, live_ref, offset_ref, v_turned, *bias_refs, places):
    me = lax.axis_index("kv")
    kv_dev = v_ref.shape[0]
    count = 2 ** len(places)
    lanes = bias_refs[0].shape[1]
    rows = lanes // GROUP
    q_dev = rows * len(bias_refs) // count
    offset = offset_ref[0]
    row = lax.broadcasted_iota(jnp.int32, (1, lanes), 1) % rows
    at_key = me * kv_dev + lax.broadcasted_iota(jnp.int32, (kv_dev, lanes), 0)
    live = live_ref[...].astype(jnp.float32)
    for c, bias_ref in enumerate(bias_refs):
        index = c * (count // len(bias_refs)) + row // q_dev
        owner = me
        for bit, place in enumerate(places):
            owner = owner ^ (((index >> bit) & 1) << place)
        token = owner * q_dev + row % q_dev
        chosen = lax.broadcasted_iota(jnp.int32, (count, lanes), 0) == owner
        seen = jnp.dot(live, chosen.astype(jnp.float32), preferred_element_type=jnp.float32)
        seen = jnp.concatenate(
            [jnp.broadcast_to(seen[b : b + 1], (BLK, lanes)) for b in range(kv_dev // BLK)], 0
        )
        allowed = (at_key <= offset + token) & ((at_key >= offset) | (seen > 0.5))
        bias_ref[...] = jnp.where(allowed, 0.0, MASKED)
    v_turned[...] = v_ref[...].T


def join_kernel(*refs):
    *in_refs, out_ref = refs
    joined = jnp.concatenate([ref[...].astype(jnp.float32) for ref in in_refs], 0)
    out_ref[...] = joined.astype(out_ref.dtype)


def join(pieces):
    rows, width = pieces[0].shape
    return pl.pallas_call(
        join_kernel,
        out_shape=jax.ShapeDtypeStruct((len(pieces) * rows, width), pieces[0].dtype),
        in_specs=[VMEM] * len(pieces),
        out_specs=VMEM,
        compiler_params=PARAMS,
    )(*pieces)


def attend_kernel(*refs, segment, first):
    q_refs, (k_ref, vt_ref, bias_ref), out_refs = refs[:-5], refs[-5:-2], refs[-2:]
    width = out_refs[0].shape[1] - STATS
    start = first * GROUP * HD
    queries_all = jnp.concatenate([ref[:, start : start + width] for ref in q_refs], 0)
    rows = queries_all.shape[0]
    chunk = rows // len(out_refs)
    kv_heads = width // (GROUP * HD)
    segments = k_ref.shape[0] // segment
    lanes = GROUP * rows
    stats = [[jnp.zeros((1, lanes), jnp.float32)] * KV_SLOT for _ in range(KINDS)]
    tiles = [(g, s) for g in range(kv_heads) for s in range(segments)]
    queries = {}

    def score(g, s):
        if g not in queries:
            queries[g] = jnp.concatenate(
                [
                    queries_all[:, (g * GROUP + h) * HD : (g * GROUP + h + 1) * HD]
                    for h in range(GROUP)
                ],
                0,
            )
        at = slice(s * segment, (s + 1) * segment)
        scores = lax.dot_general(
            k_ref[at, (first + g) * HD : (first + g + 1) * HD],
            queries[g],
            (((1,), (1,)), ((), ())),
            preferred_element_type=jnp.float32,
        )
        return scores + bias_ref[at, :]

    ahead = [score(*tile) for tile in tiles[:AHEAD]]
    for index, (g, s) in enumerate(tiles):
        if index + AHEAD < len(tiles):
            ahead.append(score(*tiles[index + AHEAD]))
        scores = ahead.pop(0)
        if s == 0:
            peaks, totals, outs = [], [], []
        peak = jnp.maximum(jnp.max(scores, 0, keepdims=True), SCORE_FLOOR * ROOT)
        weights = jnp.exp2((scores - peak) * TO_BITS)
        peaks.append(peak)
        totals.append(jnp.sum(weights, 0, keepdims=True))
        outs.append(
            jnp.dot(
                vt_ref[(first + g) * HD : (first + g + 1) * HD, s * segment : (s + 1) * segment],
                weights.astype(jnp.bfloat16),
                preferred_element_type=jnp.float32,
            )
        )
        if s < segments - 1:
            continue
        top = functools.reduce(jnp.maximum, peaks)
        scales = [jnp.exp2((peak - top) * TO_BITS) for peak in peaks]
        total = sum(e * t for e, t in zip(scales, totals))
        out = sum(e * o for e, o in zip(scales, outs))
        live = total > 0
        safe = jnp.where(live, total, 1.0)
        level = jnp.where(live, top * TO_BITS + jnp.log2(safe), NO_WEIGHT)
        out = out * jnp.where(live, 1.0 / safe, 0.0)
        largest = jnp.max(jnp.abs(out), 0, keepdims=True)
        power = jnp.clip(jnp.ceil(jnp.log2(jnp.maximum(largest, 1e-37))), -100.0, 8.0)
        out = jnp.round((out * (jnp.exp2(-power) * STEPS)).T).astype(jnp.int32)
        fixed = jnp.round(level * FIX).astype(jnp.int32)
        values = [fixed >> 16, (fixed & 0xFFFF) - 32768, power]
        for kind in range(KINDS):
            stats[kind][first + g] = values[kind].astype(jnp.float32)
        for h in range(GROUP):
            at = slice((g * GROUP + h) * HD, (g * GROUP + h + 1) * HD)
            for c, out_ref in enumerate(out_refs):
                top_row = h * rows + c * chunk
                out_ref[:, at] = out[top_row : top_row + chunk].astype(jnp.int16)
    gap = jnp.zeros((SLOT - KV_SLOT, lanes), jnp.float32)
    high, low, power = [jnp.concatenate(kind, 0) for kind in stats]
    empty = jnp.zeros((KV_SLOT, lanes), jnp.float32)
    packed = []
    for upper, lower in ((high, low), (power, empty)):
        turned = jnp.concatenate([upper, gap, lower, gap], 0).T
        packed.append(
            sum(
                pltpu.roll(turned[h * rows : (h + 1) * rows], h * KV_SLOT, 1) if h else turned[:rows]
                for h in range(GROUP)
            )
        )
    packed = jnp.concatenate(packed, 1).astype(jnp.int32)
    for c, out_ref in enumerate(out_refs):
        out_ref[:, width:] = packed[c * chunk : (c + 1) * chunk].astype(jnp.int16)


def combine_kernel(*refs, layout, heads, final):
    wide = heads * HD
    sources = []
    for number in layout:
        sources.append(refs[:number])
        refs = refs[number:]
    out_refs = refs
    copies = []
    if final:
        target, stage, sems = refs
        out_refs = [stage]
    rows = sources[0][0].shape[0]
    chunk = rows // len(out_refs)
    fixed, powers = [], []
    for source in sources:
        stats = sum(ref[:, wide // len(source) :].astype(jnp.int32) for ref in source)
        level = stats[:, :HD]
        fixed.append((level << 16) + pltpu.roll(level, SLOT, 1) + 32768)
        powers.append(stats[:, HD:].astype(jnp.float32))
    top = functools.reduce(jnp.maximum, fixed)
    weights = [jnp.exp2((f - top).astype(jnp.float32) * (1.0 / FIX)) for f in fixed]
    total = sum(weights)
    shares = [w / total for w in weights]
    amounts = [s * jnp.exp2(p) for s, p in zip(shares, powers)]
    if final:
        factors = [a * (1.0 / STEPS) for a in amounts]
    else:
        power = jnp.clip(jnp.ceil(jnp.log2(jnp.maximum(sum(amounts), 1e-37))), -100.0, 8.0)
        back = jnp.exp2(-power)
        factors = [a * back for a in amounts]
    for h in range(heads):
        at = slice(h * HD, (h + 1) * HD)
        values = []
        for source in sources:
            share = heads // len(source)
            ref, local = source[h // share], h % share
            values.append(ref[:, local * HD : (local + 1) * HD].astype(jnp.int32))
        lane = h % GROUP * KV_SLOT + h // GROUP
        out = sum(f[:, lane : lane + 1] * v.astype(jnp.float32) for f, v in zip(factors, values))
        if final:
            out = out.astype(jnp.bfloat16)
        else:
            out = jnp.round(out).astype(jnp.int32).astype(jnp.int16)
        for c, out_ref in enumerate(out_refs):
            out_ref[:, at] = out[c * chunk : (c + 1) * chunk]
        if final and (h + 1) % (heads // WRITES) == 0:
            piece = wide // WRITES
            done = pl.ds(len(copies) * piece, piece)
            copies.append(
                pltpu.make_async_copy(stage.at[:, done], target.at[:, done], sems.at[len(copies)])
            )
            copies[-1].start()
    for copy in copies:
        copy.wait()
    if not final:
        level = top + jnp.round(jnp.log2(total) * FIX).astype(jnp.int32)
        lane = lax.broadcasted_iota(jnp.int32, level.shape, 1)
        low = pltpu.roll((level & 0xFFFF) - 32768, SLOT, 1)
        packed = jnp.concatenate(
            [jnp.where(lane < SLOT, level >> 16, low), power.astype(jnp.int32)], 1
        )
        packed = packed.astype(jnp.int16)
        for c, out_ref in enumerate(out_refs):
            out_ref[:, wide:] = packed[c * chunk : (c + 1) * chunk]


def combine(sources, pieces, heads, final=False):
    rows = sources[0][0].shape[0]
    width = heads * HD + (0 if final else STATS)
    dtype = jnp.bfloat16 if final else jnp.int16
    arrays = [array for source in sources for array in source]
    return pl.pallas_call(
        functools.partial(
            combine_kernel, layout=[len(source) for source in sources], heads=heads, final=final
        ),
        out_shape=[jax.ShapeDtypeStruct((rows // pieces, width), dtype)] * pieces,
        in_specs=[VMEM] * len(arrays),
        out_specs=[pl.BlockSpec(memory_space=pl.ANY) if final else VMEM] * pieces,
        scratch_shapes=[pltpu.VMEM((rows, width), dtype), pltpu.SemaphoreType.DMA((WRITES,))]
        if final
        else [],
        compiler_params=PARAMS,
    )(*arrays)


def fetch_kernel(in_ref, out_ref, sem):
    copy = pltpu.make_async_copy(in_ref, out_ref, sem)
    copy.start()
    copy.wait()


def fetch(array):
    return pl.pallas_call(
        fetch_kernel,
        out_shape=jax.ShapeDtypeStruct(array.shape, array.dtype),
        in_specs=[pl.BlockSpec(memory_space=pl.ANY)],
        out_specs=VMEM,
        scratch_shapes=[pltpu.SemaphoreType.DMA],
        compiler_params=PARAMS,
    )(array)


def on_device(queries, keys, values, block_live, span_offset):
    count = lax.axis_size("kv")
    q_dev, q_width = queries.shape
    kv_dev, kv_width = keys.shape
    heads = q_width // HD
    steps = exchange_steps(count)
    places = []
    for deltas in steps:
        places += [(deltas[1] << b).bit_length() - 1 for b in range(len(deltas).bit_length() - 1)]
    places += [1, 0]
    parts = 2
    chunk = count * q_dev // parts

    prepared = pl.pallas_call(
        functools.partial(prep_kernel, places=places),
        out_shape=[jax.ShapeDtypeStruct((kv_width, kv_dev), values.dtype)]
        + [jax.ShapeDtypeStruct((kv_dev, chunk * GROUP), jnp.float32)] * parts,
        in_specs=[VMEM] * 2 + [pl.BlockSpec(memory_space=pltpu.SMEM)],
        out_specs=[VMEM] * (1 + parts),
        compiler_params=PARAMS,
        cost_estimate=pl.CostEstimate(flops=0, bytes_accessed=4 * 2**20, transcendentals=0),
    )(values, block_live.T, span_offset)

    block = queries
    for stage, deltas in enumerate(steps):
        others = [swap(block, d) for d in deltas[2:] + deltas[1:2]]
        if stage == 0:
            others, block = lax.optimization_barrier((others, fetch(block)))
        block = join([block] + others[-1:] + others[:-1])
    far_block, prepared = lax.optimization_barrier((swap(block, 2), prepared))
    v_turned, own_bias, other_bias = prepared

    def attend(pair, bias, part, cuts):
        width = q_width // cuts
        return pl.pallas_call(
            functools.partial(
                attend_kernel, segment=kv_dev // 2, first=part * (heads // GROUP // cuts)
            ),
            out_shape=[jax.ShapeDtypeStruct((chunk // 2, width + STATS), jnp.int16)] * 2,
            in_specs=[VMEM] * 5,
            out_specs=[VMEM] * 2,
            compiler_params=PARAMS,
            cost_estimate=pl.CostEstimate(
                flops=4 * chunk * width * kv_dev,
                bytes_accessed=4 * 2**20 // cuts,
                transcendentals=chunk * width // HD * kv_dev,
            ),
        )(*pair, keys, v_turned, bias)

    pair, other_pair = [block, far_block], [swap(block, 1), swap(far_block, 1)]
    early = attend(pair, own_bias, 0, 2)
    other_pair, early = lax.optimization_barrier((other_pair, early))
    near, far = attend(other_pair, other_bias, 0, 1)
    late = attend(pair, own_bias, 1, 2)
    late, far = lax.optimization_barrier((late, swap(far, 1)))
    (far_sum,) = combine([[early[1], late[1]], [far]], 1, heads)
    (near_sum,) = combine([[early[0], late[0]], [swap(near, 1)]], 1, heads)
    arrays = [near_sum, swap(far_sum, 2)]
    for deltas in steps[::-1]:
        outs = combine([[a] for a in arrays], len(deltas), heads)
        sent = [swap(p, d) for p, d in zip(outs[1:], deltas[1:])]
        arrays = [outs[0]] + sent[::-1]
    return combine([[a] for a in arrays], 1, heads, final=True)[0]


def solution(mesh):
    placed = (
        P(("groups", "kv"), None),
        P(("groups", "kv"), None),
        P(("groups", "kv"), None),
        P("groups", "kv"),
        P("groups"),
    )
    return jax.shard_map(
        on_device, mesh=mesh, in_specs=placed, out_specs=P(("groups", "kv"), None), check_vma=False
    )
```
